128 devices in a mesh: section: 2 (over y_lo), dp: 32 (over x, z, core), fsdp: 2 (over y_hi).
Axes of the slice: x: 4, y: 4 (y_hi: 2, y_lo: 2; y = y_hi * 2 + y_lo), z: 4, core: 2. Of those that a mesh axis runs over, the one named last changes fastest.
Arguments:
- inputs: bfloat16 [8192, 1024], P(('dp', 'fsdp')), may hold values from -6 to 6
- out_grad: bfloat16 [8192, 1024], P(('dp', 'fsdp')), may hold values from -6 to 6
- doc_lengths: int32 [128], replicated, may hold values from 1 to 128, as said below
- doc_owner: int32 [128], replicated, may hold values from 0 to 63, as said below
- loss_mask: int32 [8192], P(('dp', 'fsdp')), may hold values 0 or 1
- gain_in: bfloat16 [2, 1024], P('section', 'fsdp'), may hold values from 0.099609375 to 1.8984375
- w_in: bfloat16 [2, 1024, 3072], P('section', 'fsdp'), may hold values from -0.1875 to 0.1875
- taps: bfloat16 [2, 2048, 4], P('section', 'fsdp'), may hold values from -3 to 3
- w_decay: bfloat16 [2, 1024, 8], P('section', 'fsdp'), may hold values from -0.1875 to 0.1875
- a_log: bfloat16 [2, 4], P('section', 'fsdp'), may hold values from -4 to 0.5
- dt_bias: bfloat16 [2, 4], P('section', 'fsdp'), may hold values from -5 to -1
- gain_out: bfloat16 [2, 256], P('section', 'fsdp'), may hold values from 0.099609375 to 1.8984375
- w_out: bfloat16 [2, 1024, 1024], P('section', 'fsdp'), may hold values from -0.1875 to 0.1875
- gain_ff: bfloat16 [2, 1024], P('section', 'fsdp'), may hold values from 0.099609375 to 1.8984375
- w_ff_in: bfloat16 [2, 1024, 2816], P('section', 'fsdp'), may hold values from -0.1875 to 0.1875
- w_down: bfloat16 [2, 1408, 1024], P('section', 'fsdp'), may hold values from -0.15625 to 0.15625
Outputs:
- hidden_states: bfloat16 [2, 8192, 1024], P('section', ('dp', 'fsdp'))
- input_grads: bfloat16 [2, 8192, 1024], P('section', ('dp', 'fsdp'))
- grad_gain_in: float32 [2, 1024], P('section', 'fsdp')
- grad_w_in: float32 [2, 1024, 3072], P('section', 'fsdp')
- grad_taps: float32 [2, 2048, 4], P('section', 'fsdp')
- grad_w_decay: float32 [2, 1024, 8], P('section', 'fsdp')
- grad_a_log: float32 [2, 4], P('section', 'fsdp')
- grad_dt_bias: float32 [2, 4], P('section', 'fsdp')
- grad_gain_out: float32 [2, 256], P('section', 'fsdp')
- grad_w_out: float32 [2, 1024, 1024], P('section', 'fsdp')
- grad_gain_ff: float32 [2, 1024], P('section', 'fsdp')
- grad_w_ff_in: float32 [2, 1024, 2816], P('section', 'fsdp')
- grad_w_down: float32 [2, 1408, 1024], P('section', 'fsdp')
The draws below stay inside these ranges and needn't reach their ends.
Inputs may be any that keep to these rules, and one draw needn't show every extreme that they name: `doc_lengths`: the documents of one replica have lengths that sum to between 64 and 128; some replica holds a single document of length exactly 128. A replica may hold no document. `doc_owner`: any number of documents may go to one replica.
All inputs are finite; a program needn't handle non-finite values. No bound on the sum of `loss_mask` on one device may be relied on, other than what follows from the above.
Results may differ from the reference program's by a relative error of at most 0.03.
Values may be sent and summed in bfloat16 or wider, within the bound.
A program may use at most 256 MiB of HBM per device.

```python
import jax
import jax.numpy as jnp
from jax import lax

WIDTH = 1024
HEADS = 4
KEY_DIM = 128
VALUE_DIM = 256
HIDDEN_FF = 1408
TAPS = 4
GROUP = 64
TOK_DEV = 128
REPLICAS = 64
TOKENS = 8192
DOCS = 128
PROJ = 3072
CONV_CH = 2048
MIXED = 1024


def layout_draw(key):
    key = jax.random.fold_in(key, 7)
    key_owner, key_fill, key_piece = jax.random.split(key, 3)
    drawn_owner = jax.random.randint(key_owner, (DOCS,), 0, REPLICAS)
    first_owner = drawn_owner[0]
    positions = jnp.arange(DOCS, dtype=jnp.int32)
    clash = (drawn_owner == first_owner) & (positions > 0)
    doc_owner = jnp.where(clash, (first_owner + 1) % REPLICAS, drawn_owner).astype(jnp.int32)
    replicas = jnp.arange(REPLICAS, dtype=jnp.int32)
    replica_fill = jax.random.randint(key_fill, (REPLICAS,), TOK_DEV // 2, TOK_DEV + 1)
    replica_fill = jnp.where(replicas == first_owner, TOK_DEV, replica_fill)
    onehot = (doc_owner[:, None] == replicas[None, :]).astype(jnp.int32)
    before = jnp.cumsum(onehot, axis=0, dtype=jnp.int32) - onehot
    doc_rank = jnp.sum(before * onehot, axis=1, dtype=jnp.int32)
    counts = jnp.sum(onehot, axis=0, dtype=jnp.int32)
    held_docs = jnp.sum(onehot * counts[None, :], axis=1, dtype=jnp.int32)
    target = jnp.sum(onehot * replica_fill[None, :], axis=1, dtype=jnp.int32)
    extra_room = jnp.maximum(target - held_docs, 0) // (2 * held_docs)
    pieces = 1 + jax.random.randint(key_piece, (DOCS,), 0, 1 << 20) % (extra_room + 1)
    is_last = (doc_rank == held_docs - 1).astype(jnp.int32)
    other_lengths = pieces * (1 - is_last)
    other_sum = jnp.sum(onehot * other_lengths[:, None], axis=0, dtype=jnp.int32)
    remainder = target - jnp.sum(onehot * other_sum[None, :], axis=1, dtype=jnp.int32)
    lengths = jnp.where(is_last == 1, jnp.maximum(remainder, 1), pieces)
    return (doc_owner.astype(jnp.int32), lengths.astype(jnp.int32))


def draw_doc_lengths(key, part):
    return layout_draw(key)[1]


def draw_doc_owner(key, part):
    return layout_draw(key)[0]


def place_ends(values, own_key, smallest, largest):
    longest = values.shape.index(max(values.shape))
    spots = []
    for shift in (0, 1):
        where = [jax.random.randint(jax.random.fold_in(own_key, axis), (), 0, length) for axis, length in enumerate(values.shape)]
        where[longest] = (where[longest] + shift) % values.shape[longest]
        spots.append(tuple(where))
    return values.at[spots[0]].set(smallest).at[spots[1]].set(largest)


def shard_levels(own_key, extent, cuts, low, high):
    def one(dim, parts):
        heights = jax.random.uniform(jax.random.fold_in(jax.random.fold_in(own_key, 6), dim), (parts,), jnp.float32, low / len(cuts), high / len(cuts))
        return jnp.repeat(jnp.exp(heights), extent[dim] // parts).reshape((-1,) + (1,) * (len(extent) - dim - 1))

    level = one(*cuts[0])
    for cut in cuts[1:]:
        level = level * one(*cut)
    return level


def normal_values(rng, dims, deviation, bound, shards=(), kind=jnp.bfloat16):
    entries = jax.random.normal(rng, dims, jnp.float32) * deviation
    if len(shards) > 0:
        entries = shard_levels(rng, dims, shards, -0.22, 0.18) * entries
    return jnp.clip(entries, min=-bound, max=bound).astype(kind)


def setup_inputs(seed: int = 0) -> dict:
    key_of = jax.random.split(jax.random.key(seed), 17)
    return {
        "inputs": normal_values(key_of[0], (TOKENS, WIDTH), 1.0, 6.0, ((0, 64),)),
        "out_grad": normal_values(key_of[1], (TOKENS, WIDTH), 1.0, 6.0, ((0, 64),)),
        "doc_lengths": draw_doc_lengths(jax.random.fold_in(key_of[16], 71), 0),
        "doc_owner": draw_doc_owner(jax.random.fold_in(key_of[16], 71), 0),
        "loss_mask": place_ends((jax.random.randint(key_of[4], (TOKENS,), 0, 4) < 3).astype(jnp.int32), jax.random.fold_in(key_of[4], 1), 0, 1),
        "gain_in": jnp.clip(1.0 + 0.18 * jax.random.normal(key_of[5], (2, WIDTH), jnp.float32), 0.099609375, 1.8984375).astype(jnp.bfloat16),
        "w_in": normal_values(key_of[6], (2, WIDTH, PROJ), WIDTH ** -0.5, 0.1875, ((0, 2), (1, 2))),
        "taps": normal_values(key_of[7], (2, CONV_CH, TAPS), TAPS ** -0.5, 3.0, ((0, 2), (1, 2))),
        "w_decay": normal_values(key_of[8], (2, WIDTH, 2 * HEADS), WIDTH ** -0.5, 0.1875, ((0, 2), (1, 2))),
        "a_log": jnp.clip(-4.0 + 4.5 * jax.random.uniform(key_of[9], (2, HEADS), jnp.float32) ** shard_levels(key_of[9], (2, HEADS), ((0, 2), (1, 2)), -0.2, 0.2), -4.0, 0.5).astype(jnp.bfloat16),
        "dt_bias": jnp.clip(-5.0 + 4.0 * jax.random.uniform(key_of[10], (2, HEADS), jnp.float32) ** shard_levels(key_of[10], (2, HEADS), ((0, 2), (1, 2)), -0.2, 0.2), -5.0, -1.0).astype(jnp.bfloat16),
        "gain_out": jnp.clip(1.0 + 0.18 * jax.random.normal(key_of[11], (2, VALUE_DIM), jnp.float32), 0.099609375, 1.8984375).astype(jnp.bfloat16),
        "w_out": normal_values(key_of[12], (2, MIXED, WIDTH), MIXED ** -0.5, 0.1875, ((0, 2), (1, 2))),
        "gain_ff": jnp.clip(1.0 + 0.18 * jax.random.normal(key_of[13], (2, WIDTH), jnp.float32), 0.099609375, 1.8984375).astype(jnp.bfloat16),
        "w_ff_in": normal_values(key_of[14], (2, WIDTH, 2 * HIDDEN_FF), WIDTH ** -0.5, 0.1875, ((0, 2), (1, 2))),
        "w_down": normal_values(key_of[15], (2, HIDDEN_FF, WIDTH), HIDDEN_FF ** -0.5, 0.15625, ((0, 2), (1, 2))),
    }


EPSILON = 1e-06
FINEST_PRECISION = lax.Precision.HIGHEST

def doc_layout(doc_lengths, doc_owner, replica, length_dev):
    owned = (doc_owner == replica).astype(jnp.int32)
    doc_ends = jnp.cumsum(doc_lengths * owned, dtype=jnp.int32)
    places = jnp.arange(length_dev, dtype=jnp.int32)
    finished = (doc_ends[None, :] <= places[:, None]).astype(jnp.int32) * owned[None, :]
    segment = lax.optimization_barrier(jnp.sum(finished, axis=1, dtype=jnp.int32))
    usable = (places < doc_ends[-1]).astype(jnp.int32)
    return (segment, usable)

def rms_scale(values, gain):
    return values * lax.rsqrt(lax.optimization_barrier(jnp.mean(values * values, axis=-1, keepdims=True)) + EPSILON) * gain

def delay_rows(values, offset):
    filler = jnp.zeros((offset,) + values.shape[1:], values.dtype)
    return jnp.concatenate([filler, values[:-offset]], axis=0)

def short_conv(signal, kernel, segment):
    result = signal * kernel[:, TAPS - 1]
    for offset in range(1, TAPS):
        earlier = jnp.concatenate([jnp.full((offset,), -1, jnp.int32), segment[:-offset]])
        linked = (earlier == segment).astype(jnp.float32)
        result = result + delay_rows(signal, offset) * linked[:, None] * kernel[:, TAPS - 1 - offset]
    return result

def delta_rule(queries, keys, values, betas, logdecay, segment):
    tokens_here = queries.shape[0]
    blocks = tokens_here // GROUP

    def split(array):
        return array.reshape((blocks, GROUP) + array.shape[1:])
    strict_lower = jnp.tril(jnp.ones((GROUP, GROUP), jnp.float32), -1)
    causal = jnp.tril(jnp.ones((GROUP, GROUP), jnp.float32), 0)
    identity = jnp.eye(GROUP, dtype=jnp.float32)

    def advance(carry, block):
        running_state, last_segment = carry
        query_block, key_block, value_block, beta_block, decay_block, segment_block = block
        summed = jnp.transpose(jnp.cumsum(decay_block, axis=0))
        same_doc = (segment_block[:, None] == segment_block[None, :]).astype(jnp.float32)
        spread = summed[:, :, None] - summed[:, None, :]
        weights_pair = jnp.exp(jnp.minimum(spread, 0.0)) * same_doc[None]
        per_head_keys = jnp.transpose(key_block, (1, 0, 2))
        per_head_queries = jnp.transpose(query_block, (1, 0, 2))
        value_heads = jnp.transpose(value_block, (1, 0, 2))
        beta_heads = jnp.transpose(beta_block)
        key_gram = jnp.einsum('hik,hjk->hij', per_head_keys, per_head_keys, precision=FINEST_PRECISION)
        system = identity[None] + beta_heads[:, :, None] * key_gram * weights_pair * strict_lower[None]
        carried = (segment_block == last_segment).astype(jnp.float32)
        incoming_state = jnp.exp(summed) * carried[None, :]
        resolved_values = lax.linalg.triangular_solve(system, beta_heads[:, :, None] * value_heads, left_side=True, lower=True, unit_diagonal=True)
        resolved_keys = lax.linalg.triangular_solve(system, (beta_heads * incoming_state)[:, :, None] * per_head_keys, left_side=True, lower=True, unit_diagonal=True)
        state_updates = resolved_values - jnp.einsum('rej,rjd->red', resolved_keys, running_state, precision=FINEST_PRECISION)
        scores = jnp.einsum('hik,hjk->hij', per_head_queries, per_head_keys, precision=FINEST_PRECISION) * weights_pair * causal[None]
        output_rows = jnp.einsum('hij,hjv->hiv', scores, state_updates, precision=FINEST_PRECISION)
        output_rows = output_rows + incoming_state[:, :, None] * jnp.einsum('wru,wuq->wrq', per_head_queries, running_state, precision=FINEST_PRECISION)
        trailing_weight = jnp.exp(jnp.minimum(summed[:, -1:] - summed, 0.0)) * (segment_block == segment_block[-1]).astype(jnp.float32)[None, :]
        updated_state = (carried[-1] * jnp.exp(summed[:, -1]))[:, None, None] * running_state
        updated_state = updated_state + jnp.einsum('btu,btp->bup', trailing_weight[:, :, None] * per_head_keys, state_updates, precision=FINEST_PRECISION)
        return ((updated_state, segment_block[-1]), jnp.transpose(output_rows, (1, 0, 2)))
    start = (jnp.zeros((HEADS, KEY_DIM, VALUE_DIM), jnp.float32), jnp.int32(-1))
    _, pieces = lax.scan(advance, start, (split(queries), split(keys), split(values), split(betas), split(logdecay), split(segment)))
    return pieces.reshape(tokens_here, HEADS, VALUE_DIM)

def mixer_core(projected, decay_in, kernel, a_log, dt_bias, gain_out, segment):
    tokens_here = projected.shape[0]
    conv_width = 2 * HEADS * KEY_DIM + HEADS * VALUE_DIM
    convolved = jax.nn.silu(short_conv(projected[:, :conv_width], kernel, segment))
    queries = convolved[:, :HEADS * KEY_DIM].reshape(tokens_here, HEADS, KEY_DIM)
    keys = convolved[:, HEADS * KEY_DIM:2 * HEADS * KEY_DIM].reshape(tokens_here, HEADS, KEY_DIM)
    values = convolved[:, 2 * HEADS * KEY_DIM:].reshape(tokens_here, HEADS, VALUE_DIM)
    queries = queries * lax.rsqrt(lax.optimization_barrier(jnp.sum(queries * queries, axis=-1, keepdims=True)) + EPSILON) * KEY_DIM ** (-0.5)
    keys = keys * lax.rsqrt(lax.optimization_barrier(jnp.sum(keys * keys, axis=-1, keepdims=True)) + EPSILON)
    betas = jax.nn.sigmoid(decay_in[:, HEADS:])
    logdecay = -jnp.exp(a_log) * jax.nn.softplus(decay_in[:, :HEADS] + dt_bias)
    delta = delta_rule(queries, keys, values, betas, logdecay, segment)
    normed = rms_scale(delta, gain_out)
    gate_part = jax.nn.silu(projected[:, conv_width:]).reshape(tokens_here, HEADS, VALUE_DIM)
    return (normed * gate_part).reshape(tokens_here, HEADS * VALUE_DIM)

def layer_forward(inputs, params, segment):
    gain_in, w_in, kernel, w_decay, a_log, dt_bias, gain_out, w_out, gain_ff, w_ff_in, w_down = params
    inputs_float = inputs.astype(jnp.float32)
    normed = rms_scale(inputs_float, gain_in.astype(jnp.float32)).astype(jnp.bfloat16)
    projected = jnp.dot(normed.astype(jnp.float32), w_in.astype(jnp.float32), preferred_element_type=jnp.float32)
    decay_in = jnp.dot(normed.astype(jnp.float32), w_decay.astype(jnp.float32), preferred_element_type=jnp.float32)
    mixed = mixer_core(projected, decay_in, kernel.astype(jnp.float32), a_log.astype(jnp.float32), dt_bias.astype(jnp.float32), gain_out.astype(jnp.float32), segment).astype(jnp.bfloat16)
    middle = inputs_float + jnp.dot(mixed.astype(jnp.float32), w_out.astype(jnp.float32), preferred_element_type=jnp.float32)
    normed_ff = rms_scale(middle, gain_ff.astype(jnp.float32)).astype(jnp.bfloat16)
    gate_up = jnp.dot(normed_ff.astype(jnp.float32), w_ff_in.astype(jnp.float32), preferred_element_type=jnp.float32)
    hidden = (jax.nn.silu(gate_up[:, :HIDDEN_FF]) * gate_up[:, HIDDEN_FF:]).astype(jnp.bfloat16)
    return (middle + jnp.dot(hidden.astype(jnp.float32), w_down.astype(jnp.float32), preferred_element_type=jnp.float32)).astype(jnp.bfloat16)

def layer_backward(inputs, params, segment, cotangent):
    gain_in, w_in, kernel, w_decay, a_log, dt_bias, gain_out, w_out, gain_ff, w_ff_in, w_down = params
    inputs_float = inputs.astype(jnp.float32)
    gain_in_f = gain_in.astype(jnp.float32)
    gain_ff_f = gain_ff.astype(jnp.float32)
    normed = rms_scale(inputs_float, gain_in_f).astype(jnp.bfloat16)
    projected = jnp.dot(normed.astype(jnp.float32), w_in.astype(jnp.float32), preferred_element_type=jnp.float32)
    decay_in = jnp.dot(normed.astype(jnp.float32), w_decay.astype(jnp.float32), preferred_element_type=jnp.float32)

    def mixer_piece(proj_arg, decay_arg, kernel_arg, alog_arg, bias_arg, gain_arg):
        return mixer_core(proj_arg, decay_arg, kernel_arg, alog_arg, bias_arg, gain_arg, segment)
    mixed_float, mixer_pull = jax.vjp(mixer_piece, projected, decay_in, kernel.astype(jnp.float32), a_log.astype(jnp.float32), dt_bias.astype(jnp.float32), gain_out.astype(jnp.float32))
    mixed = mixed_float.astype(jnp.bfloat16)
    middle = inputs_float + jnp.dot(mixed.astype(jnp.float32), w_out.astype(jnp.float32), preferred_element_type=jnp.float32)
    normed_ff_float, norm_ff_pull = jax.vjp(rms_scale, middle, gain_ff_f)
    normed_ff = normed_ff_float.astype(jnp.bfloat16)
    gate_up = jnp.dot(normed_ff.astype(jnp.float32), w_ff_in.astype(jnp.float32), preferred_element_type=jnp.float32)
    gate_part = gate_up[:, :HIDDEN_FF]
    up_part = gate_up[:, HIDDEN_FF:]
    sigmoid_gate = jax.nn.sigmoid(gate_part)
    hidden = (gate_part * sigmoid_gate * up_part).astype(jnp.bfloat16)
    cot_rounded = cotangent.astype(jnp.bfloat16)
    grad_down = jnp.dot(hidden.T.astype(jnp.float32), cot_rounded.astype(jnp.float32), preferred_element_type=jnp.float32)
    d_hidden = jnp.dot(cot_rounded.astype(jnp.float32), w_down.T.astype(jnp.float32), preferred_element_type=jnp.float32)
    d_gate = d_hidden * up_part * sigmoid_gate * (1.0 + gate_part * (1.0 - sigmoid_gate))
    d_up = d_hidden * gate_part * sigmoid_gate
    d_gate_up = jnp.concatenate([d_gate, d_up], axis=1).astype(jnp.bfloat16)
    grad_ff_in = jnp.dot(normed_ff.T.astype(jnp.float32), d_gate_up.astype(jnp.float32), preferred_element_type=jnp.float32)
    d_normed_ff = jnp.dot(d_gate_up.astype(jnp.float32), w_ff_in.T.astype(jnp.float32), preferred_element_type=jnp.float32)
    d_middle_part, grad_gain_ff = norm_ff_pull(d_normed_ff)
    d_middle = cotangent + d_middle_part
    middle_rounded = d_middle.astype(jnp.bfloat16)
    grad_out = jnp.dot(mixed.T.astype(jnp.float32), middle_rounded.astype(jnp.float32), preferred_element_type=jnp.float32)
    d_mixed = jnp.dot(middle_rounded.astype(jnp.float32), w_out.T.astype(jnp.float32), preferred_element_type=jnp.float32)
    d_projected, d_decay_in, grad_kernel, grad_alog, grad_bias, grad_gain_out = mixer_pull(d_mixed)
    proj_rounded = d_projected.astype(jnp.bfloat16)
    decay_rounded = d_decay_in.astype(jnp.bfloat16)
    grad_in = jnp.dot(normed.T.astype(jnp.float32), proj_rounded.astype(jnp.float32), preferred_element_type=jnp.float32)
    grad_decay = jnp.dot(normed.T.astype(jnp.float32), decay_rounded.astype(jnp.float32), preferred_element_type=jnp.float32)
    d_normed = jnp.dot(proj_rounded.astype(jnp.float32), w_in.T.astype(jnp.float32), preferred_element_type=jnp.float32) + jnp.dot(decay_rounded.astype(jnp.float32), w_decay.T.astype(jnp.float32), preferred_element_type=jnp.float32)
    _, norm_in_pull = jax.vjp(rms_scale, inputs_float, gain_in_f)
    d_input_part, grad_gain_in = norm_in_pull(d_normed)
    d_inputs = d_middle + d_input_part
    grads = (grad_gain_in, grad_in, grad_kernel, grad_decay, grad_alog, grad_bias, grad_gain_out, grad_out, grad_gain_ff, grad_ff_in, grad_down)
    return (d_inputs, grads)

def reference(inputs, out_grad, doc_lengths, doc_owner, loss_mask, gain_in, w_in, taps, w_decay, a_log, dt_bias, gain_out, w_out, gain_ff, w_ff_in, w_down):
    weights = (gain_in, w_in, taps, w_decay, a_log, dt_bias, gain_out, w_out, gain_ff, w_ff_in, w_down)
    first_params = tuple((weight[0] for weight in weights))
    second_params = tuple((weight[1] for weight in weights))
    indices = jnp.arange(REPLICAS, dtype=jnp.int32)
    input_blocks = inputs.reshape(REPLICAS, TOK_DEV, WIDTH)
    mask_blocks = loss_mask.reshape(REPLICAS, TOK_DEV)

    def forward_with(params):

        def one_block(item):
            index, block = item
            segment, _ = doc_layout(doc_lengths, doc_owner, index, TOK_DEV)
            return layer_forward(block, params, segment)
        return one_block
    first_out = lax.map(forward_with(first_params), (indices, input_blocks))
    second_out = lax.map(forward_with(second_params), (indices, first_out))

    def backward_with(params, masked):

        def one_block(totals, item):
            index, block, cot_block, mask_block = item
            segment, usable = doc_layout(doc_lengths, doc_owner, index, TOK_DEV)
            factor = jnp.where(masked, mask_block * usable, 1).astype(jnp.float32)
            d_inputs, grads = layer_backward(block, params, segment, cot_block.astype(jnp.float32) * factor[:, None])
            return (tuple((total + grad for total, grad in zip(totals, grads))), d_inputs.astype(jnp.bfloat16))
        return one_block
    second_zero = tuple((jnp.zeros(param.shape, jnp.float32) for param in second_params))
    second_grads, second_d = lax.scan(backward_with(second_params, True), second_zero, (indices, first_out, out_grad.reshape(REPLICAS, TOK_DEV, WIDTH), mask_blocks))
    first_zero = tuple((jnp.zeros(param.shape, jnp.float32) for param in first_params))
    first_grads, first_d = lax.scan(backward_with(first_params, False), first_zero, (indices, input_blocks, second_d, mask_blocks))
    hidden_states = jnp.stack([first_out.reshape(TOKENS, WIDTH), second_out.reshape(TOKENS, WIDTH)])
    input_grads = jnp.stack([first_d.reshape(TOKENS, WIDTH), second_d.reshape(TOKENS, WIDTH)])
    stacked = tuple((jnp.stack([first_grad, second_grad]) for first_grad, second_grad in zip(first_grads, second_grads)))
    return (hidden_states, input_grads, stacked[0], stacked[1], stacked[2], stacked[3], stacked[4], stacked[5], stacked[6], stacked[7], stacked[8], stacked[9], stacked[10])
```

```python
import functools
import math

import jax
import jax.numpy as jnp
from jax import lax
from jax.experimental import pallas as pl
from jax.experimental.pallas import tpu as pltpu
from jax.sharding import PartitionSpec as P

WIDTH = 1024
HEADS = 4
KEY_DIM = 128
VALUE_DIM = 256
HIDDEN_FF = 1408
TAPS = 4
TOK = 128
PROJ = 3072
CONV = 2048
EPS = 1e-06
PACK = 80
F32 = jnp.float32
BF16 = jnp.bfloat16
HI = lax.Precision.HIGHEST
M_INV, M_FWD, M_BWD = 3, 3, None
VMEM_LIMIT = 58 * 1024 * 1024

R_GIN, R_GFF, R_GOUT, R_TAPS, R_WD, R_ALOG, R_BIAS = 0, 4, 8, 9, 41, 73, 74


def dot(a, b, dims, mode):
    if mode != 3:
        if mode is None:
            a, b = a.astype(BF16), b.astype(BF16)
        return lax.dot_general(a, b, dims, precision=mode, preferred_element_type=F32)
    a1, b1 = a.astype(BF16), b.astype(BF16)
    a2, b2 = (a - a1.astype(F32)).astype(BF16), (b - b1.astype(F32)).astype(BF16)
    one = functools.partial(lax.dot_general, dimension_numbers=dims, preferred_element_type=F32)
    return one(a1, b1) + (one(a1, b2) + one(a2, b1))


def nn(a, b, mode=None):
    return dot(a, b, (((1,), (0,)), ((), ())), mode)


def nt(a, b, mode=None):
    return dot(a, b, (((1,), (1,)), ((), ())), mode)


def tn(a, b, mode=None):
    return dot(a, b, (((0,), (0,)), ((), ())), mode)


def iota(dim, shape=(TOK, TOK)):
    return lax.broadcasted_iota(jnp.int32, shape, dim)


def sigmoid(v):
    return 1.0 / (1.0 + jnp.exp(-v))


def softplus(v):
    e = jnp.exp(-jnp.abs(v))
    u = 1.0 + e
    tail = jnp.where(u == 1.0, e, jnp.log(u) * e / jnp.where(u == 1.0, 1.0, u - 1.0))
    return jnp.maximum(v, 0.0) + tail


def lanes(sm, first, count):
    return jnp.concatenate(
        [sm[half, r : r + 1, :] for half in range(2) for r in range(first, first + count)],
        axis=1,
    )


def decay_weights(sm):
    rows = [lanes(sm, R_WD + 4 * i, 4) for i in range(8)]
    rows.append(jnp.zeros((TOK - 8, WIDTH), F32))
    return jnp.concatenate(rows, axis=0).astype(BF16)


def layout(lens, owner, replica):
    i, j = iota(0), iota(1)
    owned = (owner == replica).astype(F32)
    held = lens.astype(F32) * owned
    ends = jnp.sum(jnp.where(j <= i, held, 0.0), axis=1, keepdims=True)
    owned_col = jnp.sum(jnp.where(j == i, owned, 0.0), axis=1, keepdims=True)
    done = jnp.where(ends <= j.astype(F32), owned_col, 0.0)
    seg_row = jnp.sum(done, axis=0, keepdims=True)
    seg_col = jnp.sum(jnp.where(j == i, seg_row, 0.0), axis=1, keepdims=True)
    total = jnp.sum(held, axis=1, keepdims=True)
    t = iota(0, (TOK, 1)).astype(F32)
    usable = (t < total).astype(F32)
    return seg_col, seg_row, usable


def links(seg_col):
    wide = jnp.broadcast_to(seg_col, (TOK, TOK))
    t = iota(0)
    return [
        ((pltpu.roll(wide, d, 0) == wide) & (t >= d)).astype(F32)[:, :1] for d in range(1, TAPS)
    ]


def conv_tile(sig, taps_rows, link):
    out = sig * taps_rows[TAPS - 1]
    for d in range(1, TAPS):
        out = out + pltpu.roll(sig, d, 0) * link[d - 1] * taps_rows[TAPS - 1 - d]
    return out


def norm_rows(v):
    return lax.rsqrt(jnp.mean(v * v, axis=-1, keepdims=True) + EPS)


def decays(dec, sm):
    alog = sm[0, R_ALOG : R_ALOG + 1, :] + sm[1, R_ALOG : R_ALOG + 1, :]
    bias = sm[0, R_BIAS : R_BIAS + 1, :] + sm[1, R_BIAS : R_BIAS + 1, :]
    z = dec + bias
    rate = -jnp.exp(alog)
    logdecay = rate * softplus(z)
    tri = (iota(1) <= iota(0)).astype(F32)
    summed = nn(tri, logdecay, HI)
    return z, rate, logdecay, summed, sigmoid(dec)


def inverse(systems):
    i, j = iota(0), iota(1)
    eye = (i == j).astype(F32)
    low = i > j
    found = [eye - jnp.where(low & ((i // 2) == (j // 2)), a, 0.0) for a in systems]
    size = 2
    while size < TOK:
        mask = low & ((i // (2 * size)) == (j // (2 * size))) & ((i // size) != (j // size))
        inner = [nn(jnp.where(mask, a, 0.0), m, M_INV) for a, m in zip(systems, found)]
        found = [m - nn(m, b, M_INV) for m, b in zip(found, inner)]
        size *= 2
    return found


def head_inputs(proj, taps, link, h):
    out = []
    for first, width in (
        (KEY_DIM * h, KEY_DIM),
        (HEADS * KEY_DIM + KEY_DIM * h, KEY_DIM),
        (2 * HEADS * KEY_DIM + VALUE_DIM * h, VALUE_DIM),
    ):
        rows = [t[:, first : first + width] for t in taps]
        out.append((first, width, rows, conv_tile(proj[:, first : first + width], rows, link)))
    return out


WEIGHT_SHAPES = ((WIDTH, PROJ), (WIDTH, WIDTH), (WIDTH, 2 * HIDDEN_FF), (HIDDEN_FF, WIDTH))


def forward_body(
    x_ref, sm_ref, rows_of, out_ref, proj_ref, dec_ref, inv_ref, mid_ref, gu_ref,
    w_in, w_out, w_ff, w_down, mixed_ref, hid_ref, hook,
):
    seg_col, seg_row, _ = rows_of
    link = links(seg_col)
    same = (seg_col == seg_row).astype(F32)
    xf = x_ref[...].astype(F32)
    normed = (xf * norm_rows(xf) * lanes(sm_ref, R_GIN, 4)).astype(BF16)
    dec = nt(normed, decay_weights(sm_ref))
    dec_ref[...] = dec
    hook("in")

    @pl.loop(0, PROJ // 512)
    def _(c):
        cols = pl.ds(pl.multiple_of(c * 512, 512), 512)
        proj_ref[:, cols] = nn(normed, w_in[:, cols])

    z, rate, logdecay, summed, beta = decays(dec, sm_ref)
    summed_t = summed.T
    taps = [lanes(sm_ref, R_TAPS + 8 * k, 8) for k in range(TAPS)]
    i, j = iota(0), iota(1)
    strict = i > j
    kept, systems = [], []
    for h in range(HEADS):
        (_, _, _, qc), (_, _, _, kc), (_, _, _, vc) = head_inputs(proj_ref, taps, link, h)
        q, k, v = (c * sigmoid(c) for c in (qc, kc, vc))
        q = q * lax.rsqrt(jnp.sum(q * q, axis=-1, keepdims=True) + EPS) * KEY_DIM ** (-0.5)
        k = k * lax.rsqrt(jnp.sum(k * k, axis=-1, keepdims=True) + EPS)
        w = jnp.exp(jnp.minimum(summed[:, h : h + 1] - summed_t[h : h + 1, :], 0.0)) * same
        b = beta[:, HEADS + h : HEADS + h + 1]
        gram = nt(k, k, M_FWD)
        systems.append(jnp.where(strict, b * gram * w, 0.0))
        scores = jnp.where(i >= j, nt(q, k, M_FWD) * w, 0.0)
        kept.append((scores, b * v))
        hook(h)
    inv = inverse(systems)
    hook("inverse")
    gain_out = lanes(sm_ref, R_GOUT, 1)
    for h in range(HEADS):
        inv_ref[h] = inv[h]
        scores, bv = kept[h]
        delta = nn(scores, nn(inv[h], bv, M_FWD), M_FWD)
        cols = slice(VALUE_DIM * h, VALUE_DIM * (h + 1))
        gate = proj_ref[:, CONV + VALUE_DIM * h : CONV + VALUE_DIM * (h + 1)]
        mixed_ref[:, cols] = (
            delta * norm_rows(delta) * gain_out * (gate * sigmoid(gate))
        ).astype(BF16)
    hook("out")
    mid = xf + nn(mixed_ref[...], w_out[...])
    mid_ref[...] = mid
    normed_ff = (mid * norm_rows(mid) * lanes(sm_ref, R_GFF, 4)).astype(BF16)
    hook("ff")

    @pl.loop(0, HIDDEN_FF // 128)
    def _(c):
        a = pl.ds(pl.multiple_of(c * 128, 128), 128)
        b = pl.ds(pl.multiple_of(HIDDEN_FF + c * 128, 128), 128)
        gate = nn(normed_ff, w_ff[:, a])
        up = nn(normed_ff, w_ff[:, b])
        gu_ref[:, a] = gate
        gu_ref[:, b] = up
        hid_ref[:, a] = (gate * sigmoid(gate) * up).astype(BF16)

    hook("down")
    out_ref[...] = (mid + nn(hid_ref[...], w_down[...])).astype(BF16)


def backward_body(
    x_ref, cot_ref, sm_ref, rows_of,
    proj_ref, dec_ref, inv_ref, mid_ref, gu_ref,
    dx_ref, small_ref, nrm_t, mix_t, nff_t, hid_t, dproj_ref, dmid_ref, dgu_ref, dout_ref,
    w_in, w_out, w_ff, w_down, dmix_ref,
):
    i, j = iota(0), iota(1)
    seg_col, seg_row, _ = rows_of
    link = links(seg_col)
    same = (seg_col == seg_row).astype(F32)
    dout = cot_ref[...].astype(F32)
    doutb = dout.astype(BF16)
    dout_ref[...] = doutb
    small_ref[...] = jnp.zeros_like(small_ref)

    for c in range(HIDDEN_FF // 128):
        a = slice(c * 128, c * 128 + 128)
        b = slice(HIDDEN_FF + c * 128, HIDDEN_FF + c * 128 + 128)
        gate, up = gu_ref[:, a], gu_ref[:, b]
        sg = sigmoid(gate)
        d_hidden = nt(doutb, w_down[a, :])
        dgu_ref[:, a] = (d_hidden * up * sg * (1.0 + gate * (1.0 - sg))).astype(BF16)
        dgu_ref[:, b] = (d_hidden * gate * sg).astype(BF16)
        hid_t[a, :] = (gate * sg * up).T.astype(BF16)
    mid = mid_ref[...]
    r = norm_rows(mid)
    n = mid * r
    gain_ff = lanes(sm_ref, R_GFF, 4)
    nff_t[...] = (n * gain_ff).T.astype(BF16)

    @pl.loop(0, WIDTH // 256)
    def _(c):
        rows = pl.ds(pl.multiple_of(c * 256, 256), 256)
        dmix_ref[:, rows] = nt(dgu_ref[...], w_ff[rows, :])

    d = dmix_ref[...]
    put(small_ref, R_GFF, 4, jnp.sum(d * n, axis=0, keepdims=True))
    d = d * gain_ff
    dmid = dout + r * (d - n * jnp.mean(d * n, axis=-1, keepdims=True))
    dmidb = dmid.astype(BF16)
    dmid_ref[...] = dmidb
    dmix_ref[...] = nt(dmidb, w_out[...])

    z, rate, logdecay, summed, beta = decays(dec_ref[...], sm_ref)
    summed_t = summed.T
    taps = [lanes(sm_ref, R_TAPS + 8 * k, 8) for k in range(TAPS)]
    gain_out = lanes(sm_ref, R_GOUT, 1)
    strict, causal = i > j, i >= j
    d_gain_out = jnp.zeros((1, VALUE_DIM), F32)
    d_col = jnp.zeros((TOK, TOK), F32)
    d_row = jnp.zeros((TOK, TOK), F32)
    for h in range(HEADS):
        parts = head_inputs(proj_ref, taps, link, h)
        sig = [sigmoid(p[3]) for p in parts]
        qa, ka, v = (p[3] * s for p, s in zip(parts, sig))
        rq = lax.rsqrt(jnp.sum(qa * qa, axis=-1, keepdims=True) + EPS)
        rk = lax.rsqrt(jnp.sum(ka * ka, axis=-1, keepdims=True) + EPS)
        q = qa * rq * KEY_DIM ** (-0.5)
        k = ka * rk
        w = jnp.exp(jnp.minimum(summed[:, h : h + 1] - summed_t[h : h + 1, :], 0.0)) * same
        b = beta[:, HEADS + h : HEADS + h + 1]
        gram = nt(k, k, M_FWD)
        qk = nt(q, k, M_FWD)
        ws = jnp.where(strict, w, 0.0)
        wc = jnp.where(causal, w, 0.0)
        scores = qk * wc
        inv = inv_ref[h]
        u = nn(inv, b * v, M_FWD)
        delta = nn(scores, u, M_FWD)
        gcols = slice(CONV + VALUE_DIM * h, CONV + VALUE_DIM * (h + 1))
        vcols = slice(VALUE_DIM * h, VALUE_DIM * (h + 1))
        gate = proj_ref[:, gcols]
        sg = sigmoid(gate)
        si = gate * sg
        rd = norm_rows(delta)
        nd = delta * rd
        dm = dmix_ref[:, vcols]
        mix_t[vcols, :] = (nd * gain_out * si).T.astype(BF16)
        dproj_ref[:, gcols] = (dm * nd * gain_out * sg * (1.0 + gate * (1.0 - sg))).astype(BF16)
        dn = dm * si
        d_gain_out = d_gain_out + jnp.sum(dn * nd, axis=0, keepdims=True)
        dn = dn * gain_out
        ddelta = rd * (dn - nd * jnp.mean(dn * nd, axis=-1, keepdims=True))
        dscores = nt(ddelta, u, M_BWD)
        du = tn(scores, ddelta, M_BWD)
        dr = tn(inv, du, M_BWD)
        da = -nt(dr, u, M_BWD)
        dqk = dscores * wc
        dgram = da * b * ws
        pair = dqk * qk + dgram * gram
        dq = nn(dqk, k, M_BWD)
        dk = tn(dqk, q, M_BWD) + nn(dgram + dgram.T, k, M_BWD)
        dv = b * dr
        dbeta = jnp.sum(da * gram * ws, axis=1, keepdims=True) + jnp.sum(
            dr * v, axis=1, keepdims=True
        )
        d_col = jnp.where(j == h, jnp.sum(pair, axis=1, keepdims=True), d_col)
        d_col = jnp.where(j == HEADS + h, dbeta, d_col)
        d_row = jnp.where(i == h, jnp.sum(pair, axis=0, keepdims=True), d_row)
        dq = KEY_DIM ** (-0.5) * dq
        dqa = rq * dq - qa * (rq * rq * rq) * jnp.sum(dq * qa, axis=-1, keepdims=True)
        dka = rk * dk - ka * (rk * rk * rk) * jnp.sum(dk * ka, axis=-1, keepdims=True)
        for (first, width, rows, c), s, dact in zip(parts, sig, (dqa, dka, dv)):
            dc = dact * s * (1.0 + c * (1.0 - s))
            raw = proj_ref[:, first : first + width]
            total = dc * rows[TAPS - 1]
            put_taps(small_ref, TAPS - 1, first, jnp.sum(dc * raw, axis=0, keepdims=True))
            for dist in range(1, TAPS):
                dcl = dc * link[dist - 1]
                put_taps(
                    small_ref, TAPS - 1 - dist, first,
                    jnp.sum(dcl * pltpu.roll(raw, dist, 0), axis=0, keepdims=True),
                )
                total = total + pltpu.roll(dcl, TOK - dist, 0) * rows[TAPS - 1 - dist]
            dproj_ref[:, first : first + width] = total.astype(BF16)
    put(small_ref, R_GOUT, 1, d_gain_out)
    d_summed = d_col - d_row.T
    later = (j >= i).astype(F32)
    dlog = nn(later, d_summed, HI)
    dz = dlog * rate * sigmoid(z)
    head_lane = j < HEADS
    d_alog = jnp.sum(jnp.where(head_lane, dlog * logdecay, 0.0), axis=0, keepdims=True)
    d_bias = jnp.sum(jnp.where(head_lane, dz, 0.0), axis=0, keepdims=True)
    for half in range(2):
        small_ref[half, R_ALOG : R_ALOG + 1, :] = d_alog
        small_ref[half, R_BIAS : R_BIAS + 1, :] = d_bias
    ddec = jnp.where(
        head_lane, dz, jnp.where(j < 2 * HEADS, d_col * beta * (1.0 - beta), 0.0)
    ).astype(BF16)

    xf = x_ref[...].astype(F32)
    r = norm_rows(xf)
    n = xf * r
    gain_in = lanes(sm_ref, R_GIN, 4)
    normed = (n * gain_in).astype(BF16)
    nrm_t[...] = (n * gain_in).T.astype(BF16)
    gwd = tn(ddec, normed)
    for row in range(2 * HEADS):
        put(small_ref, R_WD + 4 * row, 4, gwd[row : row + 1, :])

    @pl.loop(0, WIDTH // 256)
    def _(c):
        rows = pl.ds(pl.multiple_of(c * 256, 256), 256)
        dmix_ref[:, rows] = nt(dproj_ref[...], w_in[rows, :])

    d = dmix_ref[...] + nn(ddec, decay_weights(sm_ref))
    put(small_ref, R_GIN, 4, jnp.sum(d * n, axis=0, keepdims=True))
    d = d * gain_in
    dx_ref[...] = (dmid + r * (d - n * jnp.mean(d * n, axis=-1, keepdims=True))).astype(BF16)


def put(ref, first, count, row):
    for half in range(2):
        for c in range(count):
            at = (half * count + c) * 128
            ref[half, first + c : first + c + 1, :] = row[:, at : at + 128]


def put_taps(ref, tap, first, row):
    for c in range(row.shape[1] // 128):
        block = first // 128 + c
        at = R_TAPS + 8 * tap + block % 8
        ref[block // 8, at : at + 1, :] = row[:, c * 128 : c * 128 + 128]


ORDERS = ((0, 1, 2, 3), (1, 0, 3, 2), (2, 3, 0, 1), (3, 2, 1, 0))
FLAT = (
    (2, 0, 768, 0, True), (2, 768, 768, 1, True), (2, 1536, 768, 3, True), (2, 2304, 512, 2, True),
    (3, 0, 1024, 2, False), (0, 0, 1024, 0, False), (0, 1024, 1024, 1, False),
    (0, 2048, 1024, 3, False), (1, 0, 256, 0, False), (1, 256, 512, 1, False),
    (1, 768, 256, 3, False),
)
DOWN = 3


class Place:
    def __init__(self):
        self.section = lax.axis_index("section")
        dp = lax.axis_index("dp")
        self.half = lax.axis_index("fsdp")
        x, z, core = dp // 8, (dp // 2) % 4, dp % 2
        self.core = core

        def at(x, z, core, half):
            return (self.section, (x * 4 + z) * 2 + core, half)

        xa, za = x + 1 - 2 * (x % 2), z + 1 - 2 * (z % 2)
        self.links = (
            at(xa, z, core, self.half),
            at(3 - x, z, core, self.half),
            at(x, za, core, self.half),
            at(x, 3 - z, core, self.half),
        )
        self.sibling = at(x, z, 1 - core, self.half)
        self.pair = at(x, z, core, 1 - self.half)
        self.other = (1 - self.section, dp, self.half)
        self.bits = ((x % 2 + x // 2) % 2, x // 2, (z % 2 + z // 2) % 2, z // 2)

    def greet(self, *more):
        barrier = pltpu.get_barrier_semaphore()
        everyone = (*self.links, self.sibling, self.pair, *more)
        for device in everyone:
            pl.semaphore_signal(
                barrier, inc=1, device_id=device, device_id_type=pl.DeviceIdType.MESH
            )
        pl.semaphore_wait(barrier, len(everyone))


class Chunk:
    def __init__(self, place, weight, first, width, flavor, pair_first=False):
        self.pair_first = pair_first
        self.weight, self.first, self.width, self.order = weight, first, width, ORDERS[flavor]
        self.bits = [place.bits[d] for d in self.order]
        self.partners = [place.links[d] for d in self.order]
        self.rows = 352 if weight == DOWN else 256

    def size(self, steps):
        if self.weight == DOWN:
            return (self.rows >> min(steps, 1), self.width >> max(steps - 1, 0))
        return (self.rows >> steps, self.width)

    def start(self, steps, other=False):
        row = col = 0
        for k in range(1, steps + 1):
            bit = self.bits[k - 1]
            if other and k == steps:
                bit = 1 - bit
            if self.weight == DOWN and k > 1:
                col = col + bit * self.size(k)[1]
            else:
                row = row + bit * self.size(k)[0]
        return row, col

    def window(self, steps, other=False, row0=0, col0=0):
        (row, col), (rows, cols) = self.start(steps, other), self.size(steps)
        row, col = row + row0, col + col0
        if not isinstance(row, int):
            row = pl.multiple_of(row, 16)
        if not isinstance(col, int):
            col = pl.multiple_of(col, 128)
        return pl.ds(row, rows), pl.ds(col, cols)


def send(src, dst, sems, k, device):
    copy = pltpu.make_async_remote_copy(
        src_ref=src, dst_ref=dst, send_sem=sems[0].at[k], recv_sem=sems[1].at[k],
        device_id=device, device_id_type=pl.DeviceIdType.MESH,
    )
    copy.start()
    return copy


HALF_ROWS = (512, 512, 512, 704)
COLUMNS = (PROJ, WIDTH, 2 * HIDDEN_FF, WIDTH)


GATHER_FLAT = tuple(
    c[:4] for c in sorted(FLAT, key=lambda c: (0, 3, 1, 2)[c[0]])
)
PAIR_LAG = 1.0


def in_order(stages, lag):
    found = []
    for n, c in enumerate(FLAT):
        for stage in range(stages):
            late = lag if c[4] and stage else 0.0
            found.append((stage + late, n, stage))
    return [(n, stage) for _, n, stage in sorted(found)]


PACKED = 0
STAGES = 6


def layers_kernel(
    x_ref, cot_ref, mask_ref, lens_ref, own_ref,
    gin_ref, gff_ref, gout_ref, taps_ref, wdec_ref, alog_ref, bias_ref, wi, wo, wf, wd,
    out_ref, dx_ref, small_ref, nrm_t, mix_t, nff_t, hid_t, dproj_ref, dmid_ref, dgu_ref, dout_ref,
    w_in, w_out, w_ff, w_down, sm_ref, pk_wide, pk_ref, pk_far, proj_ref, dec_ref, inv_ref,
    mid_ref, gu_ref, mixed_ref, hid_ref, dmix_ref, xin_ref, next_ref, cin_ref, back_ref,
    send_sem, recv_sem, local_sem,
):
    place = Place()
    pk_wide[...] = jnp.zeros_like(pk_wide)
    for ref, first, per_row in (
        (gin_ref, R_GIN, 4), (gff_ref, R_GFF, 4), (gout_ref, R_GOUT, 1), (taps_ref, R_TAPS, 8),
        (wdec_ref, R_WD, 4),
    ):
        rows = ref[...].astype(F32)
        for r in range(rows.shape[0]):
            for c in range(per_row):
                at = first + r * per_row + c
                pk_wide[at : at + 1, :] = rows[r : r + 1, c * 128 : c * 128 + 128]
    for ref, at in ((alog_ref, R_ALOG), (bias_ref, R_BIAS)):
        two = ref[...].astype(F32)
        none = jnp.zeros((1, 2), F32)
        pk_wide[at : at + 1, 0:2] = jnp.where(place.half == 0, two, none)
        pk_wide[at : at + 1, 2:4] = jnp.where(place.half == 0, none, two)
    pk_ref[...] = pk_wide[...].astype(BF16)
    sems = (send_sem, recv_sem)
    shards, whole = (wi, wo, wf, wd), (w_in, w_out, w_ff, w_down)
    chunks = [Chunk(place, *c) for c in GATHER_FLAT]
    count = len(chunks)
    first = {w: [n for n, c in enumerate(chunks) if c.weight == w] for w in range(4)}

    def make(src, dst, k, device):
        return pltpu.make_async_remote_copy(
            src_ref=src, dst_ref=dst, send_sem=sems[0].at[k], recv_sem=sems[1].at[k],
            device_id=device, device_id_type=pl.DeviceIdType.MESH,
        )

    def local(w):
        rows = HALF_ROWS[w]
        at = pl.ds(pl.multiple_of(place.half * rows, 16), rows)
        return pltpu.make_async_copy(shards[w], whole[w].at[at, :], local_sem.at[w])

    def stage_copy(n, stage):
        c = chunks[n]
        w, rows = c.weight, HALF_ROWS[c.weight]
        k = 1 + stage * count + n
        if stage == 0:
            src = shards[w].at[c.window(4, row0=place.core * c.rows, col0=c.first)]
            to = c.window(4, row0=place.half * rows + place.core * c.rows, col0=c.first)
            return make(src, whole[w].at[to], k, place.pair)
        row0 = (1 - place.half) * rows + place.core * c.rows
        block = whole[w].at[c.window(5 - stage, row0=row0, col0=c.first)]
        device = c.partners[4 - stage] if stage < 5 else place.sibling
        return make(block, block, k, device)

    def passed_on(ns, stage):
        for n in ns:
            stage_copy(n, stage - 1).wait_recv()
            stage_copy(n, stage).start()

    rest = first[1] + first[2] + first[3]

    def complete(w):
        for n in first[w]:
            stage_copy(n, STAGES - 1).wait_recv()
        local(w).wait()

    def gather_hook(point):
        if point == "in":
            for stage in range(1, 4):
                passed_on(first[0], stage)
                if stage == 1:
                    passed_on(rest, 1)
            passed_on(first[0], 4)
            passed_on(rest, 2)
            passed_on(first[0], 5)
            complete(0)
        elif point == 0:
            passed_on(rest, 3)
        elif point == 2:
            passed_on(rest, 4)
        elif point == "inverse":
            passed_on(rest, 5)
        elif point in ("out", "ff", "down"):
            complete({"out": 1, "ff": 2, "down": 3}[point])

    place.greet(place.other)
    packed = make(pk_ref, pk_far, PACKED, place.pair)
    packed.start()
    for w in (0, 1, 2, 3):
        for n in first[w]:
            stage_copy(n, 0).start()
        local(w).start()
    rows_of = layout(lens_ref[...], own_ref[...], lax.axis_index("dp") * 2 + place.half)
    packed.wait()
    sm_ref[place.half] = pk_ref[...].astype(F32)
    sm_ref[1 - place.half] = pk_far[...].astype(F32)
    xin_ref[...] = x_ref[...]
    forth = make(out_ref, next_ref, 1 + STAGES * count, place.other)
    back = make(dx_ref, back_ref, 2 + STAGES * count, place.other)
    section = place.section

    @pl.loop(0, 2)
    def _(turn):
        def hook(point):
            @pl.when(turn == 0)
            def _():
                gather_hook(point)

        forward_body(
            xin_ref, sm_ref, rows_of, out_ref, proj_ref, dec_ref, inv_ref, mid_ref, gu_ref,
            w_in, w_out, w_ff, w_down, mixed_ref, hid_ref, hook,
        )

        @pl.when(turn == 0)
        def _():
            forth.start()
            forth.wait()
            xin_ref[...] = jnp.where(section == 0, x_ref[...], next_ref[...])

    mask = jnp.sum(
        jnp.where(iota(0) == iota(1), mask_ref[...].astype(F32), 0.0), axis=1, keepdims=True
    )
    cin_ref[...] = (cot_ref[...].astype(F32) * (mask * rows_of[2])).astype(BF16)

    @pl.loop(0, 2)
    def _(turn):
        backward_body(
            xin_ref, cin_ref, sm_ref, rows_of,
            proj_ref, dec_ref, inv_ref, mid_ref, gu_ref,
            dx_ref, small_ref, nrm_t, mix_t, nff_t, hid_t, dproj_ref, dmid_ref, dgu_ref, dout_ref,
            w_in, w_out, w_ff, w_down, dmix_ref,
        )

        @pl.when(turn == 0)
        def _():
            back.start()
            back.wait()
            cin_ref[...] = jnp.where(section == 0, back_ref[...], cin_ref[...])

    for n in range(count):
        for stage in range(STAGES):
            stage_copy(n, stage).wait_send()


def layers(x, cot, mask, lens, own, smalls, weights):
    vm = pl.BlockSpec(memory_space=pltpu.VMEM)
    hbm = pl.BlockSpec(memory_space=pl.ANY)
    tokens = (TOK, WIDTH)
    shapes = [
        (tokens, BF16), (tokens, BF16), ((2, PACK, 128), F32), ((WIDTH, TOK), BF16),
        ((WIDTH, TOK), BF16), ((WIDTH, TOK), BF16), ((HIDDEN_FF, TOK), BF16), ((TOK, PROJ), BF16),
        (tokens, BF16), ((TOK, 2 * HIDDEN_FF), BF16), (tokens, BF16),
    ]
    scratch = [(s, BF16) for s in WEIGHT_SHAPES] + [
        ((2, PACK, 128), F32), ((PACK, 128), F32), ((PACK, 128), BF16), ((PACK, 128), BF16),
        ((TOK, PROJ), F32), ((TOK, TOK), F32), ((HEADS, TOK, TOK), F32), (tokens, F32),
        ((TOK, 2 * HIDDEN_FF), F32), (tokens, BF16), ((TOK, HIDDEN_FF), BF16), (tokens, F32),
        (tokens, BF16), (tokens, BF16), (tokens, BF16), (tokens, BF16),
    ]
    count = 3 + STAGES * len(GATHER_FLAT)
    return pl.pallas_call(
        layers_kernel,
        name="gather_and_layers",
        out_shape=[jax.ShapeDtypeStruct(s, d) for s, d in shapes],
        in_specs=[vm] * 12 + [hbm] * 4,
        out_specs=[vm] * len(shapes),
        scratch_shapes=[pltpu.VMEM(s, d) for s, d in scratch]
        + [
            pltpu.SemaphoreType.DMA((count,)),
            pltpu.SemaphoreType.DMA((count,)),
            pltpu.SemaphoreType.DMA((4,)),
        ],
        compiler_params=pltpu.CompilerParams(
            collective_id=1, has_side_effects=True, vmem_limit_bytes=VMEM_LIMIT
        ),
    )(x, cot, mask, lens, own, *smalls, *weights)


def reduce_kernel(
    lag, stages, small_ref, l_in, l_out, l_ff, l_down, r_in, r_out, r_ff, r_down,
    tot_ref, g_in, g_out, g_ff, g_down, *scratch,
):
    place = Place()
    lhs, rhs = (l_in, l_out, l_ff, l_down), (r_in, r_out, r_ff, r_down)
    grads = (g_in, g_out, g_ff, g_down)
    peer_l, peer_r = scratch[0:4], scratch[4:8]
    count = len(FLAT)
    parts, fins = scratch[8 : 8 + count], scratch[8 + count : 8 + 2 * count]
    scratch = scratch[8 + 2 * count :]
    arrived = [scratch[5 * n : 5 * n + 5] for n in range(count)]
    sums, sums_in, sums_pair, send_sem, recv_sem, local_sem = scratch[5 * count :]
    sems = (send_sem, recv_sem)
    ids = iter(range(10 * count + 18))
    place.greet()
    sent = []

    crossing = {}
    for w in (2, 3, 0, 1):
        rows = peer_l[w].shape[1]
        found = []
        for h in range(2):
            at = pl.multiple_of(HALF_ROWS[w] * h + (1 - place.core) * rows, 16)
            found.append(
                send(lhs[w].at[pl.ds(at, rows), :], peer_l[w].at[h], sems, next(ids), place.sibling)
            )
        found.append(send(rhs[w], peer_r[w], sems, next(ids), place.sibling))
        sent += found
        crossing[w] = found

    sums[0] = small_ref[...]
    steps = (place.sibling, *place.links)
    small_ids = [next(ids) for _ in range(6)]
    small = send(sums.at[0], sums_in.at[0], sems, small_ids[0], steps[0])
    sent.append(small)

    chunks = [Chunk(place, *c) for c in FLAT]
    last, local = {}, {}

    def product(n, first):
        c = chunks[n]
        w = c.weight
        if c.pair_first:
            half = 1 - place.half if first else place.half
            blocks, rows = [(half, 0)], c.rows
        else:
            offset = pl.multiple_of(c.start(1, first)[0], 16)
            blocks, rows = [(0, offset), (1, offset)], c.size(1)[0]
        left = []
        for h, offset in blocks:
            at = pl.multiple_of(HALF_ROWS[w] * h + place.core * c.rows + offset, 16)
            left.append(
                jnp.concatenate(
                    [lhs[w][pl.ds(at, rows), :], peer_l[w][h, pl.ds(offset, rows), :]], axis=1
                )
            )
        both = left[0] if len(left) == 1 else jnp.concatenate(left, axis=0)
        for t in range(0, c.width, 256):
            cols = slice(c.first + t, c.first + t + 256)
            right = jnp.concatenate([rhs[w][:, cols], peer_r[w][:, cols]], axis=0)
            out = nn(both, right).astype(BF16)
            for k, (h, offset) in enumerate(blocks):
                parts[n][h, pl.ds(offset, rows), t : t + 256] = out[k * rows : (k + 1) * rows]

    def halves(n):
        return place.half if chunks[n].pair_first else slice(None)

    def give(n, step):
        c = chunks[n]
        at = c.window(step, other=True)
        last[n] = send(
            parts[n].at[halves(n), at[0], at[1]], arrived[n][step - 1], sems, next(ids),
            c.partners[step - 1],
        )
        sent.append(last[n])

    def add(n, step):
        c = chunks[n]
        (row, col), (rows, cols) = c.start(step), c.size(step)
        col = pl.ds(pl.multiple_of(col, 128), cols) if c.weight == DOWN else slice(None)
        lead = (slice(None),) if not c.pair_first else ()

        @pl.loop(0, rows // 16)
        def _(t):
            at = pl.ds(pl.multiple_of(row + t * 16, 16), 16)
            got = arrived[n][step - 1][(*lead, pl.ds(pl.multiple_of(t * 16, 16), 16), slice(None))]
            old = parts[n][halves(n), at, col]
            parts[n][halves(n), at, col] = (old.astype(F32) + got.astype(F32)).astype(BF16)

    def finish(n, block):
        c = chunks[n]
        fins[n][...] = block
        to = grads[c.weight].at[c.window(4, row0=place.core * c.rows, col0=c.first)]
        local[n] = pltpu.make_async_copy(fins[n], to, local_sem.at[n])
        local[n].start()
        last[n] = send(fins[n], to, sems, next(ids), c.partners[3])
        sent.append(last[n])

    def to_pair(n, src, dst):
        last[n] = send(src, dst, sems, next(ids), place.pair)
        sent.append(last[n])

    for n, stage in in_order(stages, lag):
        c = chunks[n]
        w = c.weight
        if stage == 0:
            for copy in crossing.pop(w, ()):
                copy.wait_recv()
            product(n, True)
            if c.pair_first:
                to_pair(n, parts[n].at[1 - place.half], arrived[n][4])
            else:
                give(n, 1)
            product(n, False)
        elif c.pair_first and stage == 1:
            last[n].wait_recv()

            @pl.loop(0, c.rows // 16)
            def _(t):
                at = pl.ds(pl.multiple_of(t * 16, 16), 16)
                old = parts[n][place.half, at, :].astype(F32)
                parts[n][place.half, at, :] = (old + arrived[n][4][at, :].astype(F32)).astype(BF16)

            give(n, 1)
        elif c.pair_first and stage <= 4:
            last[n].wait_recv()
            add(n, stage - 1)
            give(n, stage)
        elif c.pair_first and stage == 5:
            last[n].wait_recv()
            at = c.window(4)
            finish(
                n,
                (
                    parts[n][place.half, at[0], at[1]].astype(F32)
                    + arrived[n][3][...].astype(F32)
                ).astype(BF16),
            )
        elif stage <= 3:
            last[n].wait_recv()
            add(n, stage)
            give(n, stage + 1)
        elif stage == 4:
            last[n].wait_recv()
            add(n, 4)
            at = c.window(4)
            to_pair(n, parts[n].at[1 - place.half, at[0], at[1]], arrived[n][4])
        elif stage == 5:
            last[n].wait_recv()
            at = c.window(4)
            finish(
                n,
                (
                    parts[n][place.half, at[0], at[1]].astype(F32)
                    + arrived[n][4][...].astype(F32)
                ).astype(BF16),
            )
        elif stage <= 8:
            if stage == 6:
                local[n].wait()
            last[n].wait_recv()
            steps_left = 9 - stage
            block = grads[w].at[c.window(steps_left, row0=place.core * c.rows, col0=c.first)]
            last[n] = send(block, block, sems, next(ids), c.partners[steps_left - 1])
            sent.append(last[n])
        else:
            last[n].wait_recv()
            block = grads[w].at[c.window(0, row0=place.core * c.rows, col0=c.first)]
            last[n] = send(block, block, sems, next(ids), place.sibling)
            sent.append(last[n])
        if stage == 0 and 1 <= n <= 5:
            small.wait_recv()
            sums[n] = sums[n - 1] + sums_in[n - 1]
            if n < 5:
                small = send(sums.at[n], sums_in.at[n], sems, small_ids[n], steps[n])
            else:
                small = send(
                    sums.at[5, 1 - place.half], sums_pair, sems, small_ids[5], place.pair
                )
            sent.append(small)
    small.wait_recv()
    tot_ref[...] = sums[5, place.half] + sums_pair[...]
    for n in range(count):
        last[n].wait_recv()
    for copy in sent:
        copy.wait_send()


class Sizes:
    bits = (0, 0, 0, 0)
    links = (None,) * 4


def reduce(small, lhs, rhs, lag=None, stages=10, cid=2):
    vm = pl.BlockSpec(memory_space=pltpu.VMEM)
    hbm = pl.BlockSpec(memory_space=pl.ANY)
    chunks = [Chunk(Sizes, *c) for c in FLAT]
    count = len(FLAT)
    scratch = [pltpu.VMEM((2, r // 2, TOK), BF16) for r in HALF_ROWS]
    scratch += [pltpu.VMEM((TOK, c), BF16) for c in COLUMNS]
    scratch += [pltpu.VMEM((2, *c.size(0)), BF16) for c in chunks]
    scratch += [pltpu.VMEM(c.size(4), BF16) for c in chunks]
    for c in chunks:
        lead = () if c.pair_first else (2,)
        scratch += [pltpu.VMEM((*lead, *c.size(k)), BF16) for k in range(1, 5)]
        scratch.append(pltpu.VMEM(c.size(0 if c.pair_first else 4), BF16))
    total = 10 * count + 18
    scratch += [
        pltpu.VMEM((6, 2, PACK, 128), F32),
        pltpu.VMEM((5, 2, PACK, 128), F32),
        pltpu.VMEM((PACK, 128), F32),
        pltpu.SemaphoreType.DMA((total,)),
        pltpu.SemaphoreType.DMA((total,)),
        pltpu.SemaphoreType.DMA((count,)),
    ]
    return pl.pallas_call(
        functools.partial(reduce_kernel, PAIR_LAG if lag is None else lag, stages),
        name="reduce_gradients",
        out_shape=[jax.ShapeDtypeStruct((PACK, 128), F32)]
        + [jax.ShapeDtypeStruct((r, c), BF16) for r, c in zip(HALF_ROWS, COLUMNS)],
        in_specs=[vm] * 9,
        out_specs=[vm] + [hbm] * 4,
        scratch_shapes=scratch,
        compiler_params=pltpu.CompilerParams(
            collective_id=cid, has_side_effects=True, vmem_limit_bytes=VMEM_LIMIT
        ),
    )(small, *lhs, *rhs)


def finish_kernel(tot_ref, *refs):
    sources, (o_gin, o_taps, o_wd, o_alog, o_bias, o_gout, o_gff) = refs[:4], refs[4:11]
    targets, narrow, wide = refs[11:15], refs[15:19], refs[19:23]
    in_sem, out_sem = refs[23:]
    half = lax.axis_index("fsdp")
    blocks = []
    for w, rows in enumerate(HALF_ROWS):
        size = rows // 4
        blocks += [(w, slice(k * size, (k + 1) * size)) for k in range(4)]
    loads = [
        pltpu.make_async_copy(sources[w].at[at], narrow[w].at[at], in_sem.at[k])
        for k, (w, at) in enumerate(blocks)
    ]
    for copy in loads:
        copy.start()

    def row(first, count):
        return jnp.concatenate([tot_ref[first + k : first + k + 1, :] for k in range(count)], 1)

    o_gin[...] = row(R_GIN, 4)
    o_gff[...] = row(R_GFF, 4)
    o_gout[...] = row(R_GOUT, 1)
    for k in range(TAPS):
        o_taps[k : k + 1, :] = row(R_TAPS + 8 * k, 8)
    for k in range(2 * HEADS):
        o_wd[k : k + 1, :] = row(R_WD + 4 * k, 4)
    for ref, at in ((o_alog, R_ALOG), (o_bias, R_BIAS)):
        both = row(at, 1)
        ref[...] = jnp.where(half == 0, both[:, 0:2], both[:, 2:4])
    stores = []
    for k, (w, at) in enumerate(blocks):
        loads[k].wait()
        first, count = at.start, at.stop - at.start

        @pl.loop(0, count // 16)
        def _(t):
            here = pl.ds(pl.multiple_of(first + t * 16, 16), 16)
            wide[w][here, :] = narrow[w][here, :].astype(F32)

        copy = pltpu.make_async_copy(wide[w].at[at], targets[w].at[at], out_sem.at[k])
        copy.start()
        stores.append(copy)
    for copy in stores:
        copy.wait()


def finished(total, grads):
    vm = pl.BlockSpec(memory_space=pltpu.VMEM)
    hbm = pl.BlockSpec(memory_space=pl.ANY)
    small = [(1, 512), (TAPS, 1024), (2 * HEADS, 512), (1, 2), (1, 2), (1, 128), (1, 512)]
    shapes = list(zip(HALF_ROWS, COLUMNS))
    return pl.pallas_call(
        finish_kernel,
        name="widen_gradients",
        out_shape=[jax.ShapeDtypeStruct(s, F32) for s in small + shapes],
        in_specs=[vm] + [hbm] * 4,
        out_specs=[vm] * 7 + [hbm] * 4,
        scratch_shapes=[pltpu.VMEM(s, BF16) for s in shapes]
        + [pltpu.VMEM(s, F32) for s in shapes]
        + [pltpu.SemaphoreType.DMA((16,)), pltpu.SemaphoreType.DMA((16,))],
        compiler_params=pltpu.CompilerParams(vmem_limit_bytes=VMEM_LIMIT),
    )(total, *grads)


def on_device(
    inputs, out_grad, doc_lengths, doc_owner, loss_mask, gain_in, w_in, taps, w_decay, a_log,
    dt_bias, gain_out, w_out, gain_ff, w_ff_in, w_down,
):
    lens, own, mask = (a.reshape(1, TOK) for a in (doc_lengths, doc_owner, loss_mask))
    smalls = (gain_in, gain_ff, gain_out, taps[0].T, w_decay[0].T, a_log, dt_bias)
    mine = (w_in[0], w_out[0], w_ff_in[0], w_down[0])
    out, dx, small, nrm_t, mix_t, nff_t, hid_t, dproj, dmid, dgu, dout = layers(
        inputs, out_grad, mask, lens, own, smalls, mine
    )
    total, *grads = reduce(small, (nrm_t, mix_t, nff_t, hid_t), (dproj, dmid, dgu, dout))
    gin, g_taps, g_wd, g_alog, g_bias, g_gout, g_gff, g_in, g_out, g_ff, g_down = finished(
        total, grads
    )
    return (
        out[None], dx[None], gin, g_in[None], g_taps.T[None], g_wd.T[None], g_alog, g_bias, g_gout,
        g_out[None], g_gff, g_ff[None], g_down[None],
    )


def solution(mesh):
    tokens, pair = P(("dp", "fsdp"), None), P("section", "fsdp")
    matrix = P("section", "fsdp", None)
    params = (pair, matrix, matrix, matrix, pair, pair, pair, matrix, pair, matrix, matrix)
    return jax.shard_map(
        on_device,
        mesh=mesh,
        in_specs=(tokens, tokens, P(), P(), P(("dp", "fsdp")), *params),
        out_specs=(P("section", ("dp", "fsdp"), None),) * 2 + params,
        check_vma=False,
    )
```

```python
import functools
import math

import jax
import jax.numpy as jnp
from jax import lax
from jax.experimental import pallas as pl
from jax.experimental.pallas import tpu as pltpu
from jax.sharding import PartitionSpec as P

WIDTH = 1024
HEADS = 4
KEY_DIM = 128
VALUE_DIM = 256
HIDDEN_FF = 1408
TAPS = 4
TOK = 128
PROJ = 3072
CONV = 2048
EPS = 1e-06
PACK = 80
F32 = jnp.float32
BF16 = jnp.bfloat16
HI = lax.Precision.HIGHEST
M_INV, M_FWD, M_BWD = 3, 3, None
VMEM_LIMIT = 58 * 1024 * 1024

R_GIN, R_GFF, R_GOUT, R_TAPS, R_WD, R_ALOG, R_BIAS = 0, 4, 8, 9, 41, 73, 74


def dot(a, b, dims, mode):
    if mode != 3:
        if mode is None:
            a, b = a.astype(BF16), b.astype(BF16)
        return lax.dot_general(a, b, dims, precision=mode, preferred_element_type=F32)
    a1, b1 = a.astype(BF16), b.astype(BF16)
    a2, b2 = (a - a1.astype(F32)).astype(BF16), (b - b1.astype(F32)).astype(BF16)
    one = functools.partial(lax.dot_general, dimension_numbers=dims, preferred_element_type=F32)
    return one(a1, b1) + (one(a1, b2) + one(a2, b1))


def nn(a, b, mode=None):
    return dot(a, b, (((1,), (0,)), ((), ())), mode)


def nt(a, b, mode=None):
    return dot(a, b, (((1,), (1,)), ((), ())), mode)


def tn(a, b, mode=None):
    return dot(a, b, (((0,), (0,)), ((), ())), mode)


def iota(dim, shape=(TOK, TOK)):
    return lax.broadcasted_iota(jnp.int32, shape, dim)


def sigmoid(v):
    return 1.0 / (1.0 + jnp.exp(-v))


def softplus(v):
    e = jnp.exp(-jnp.abs(v))
    u = 1.0 + e
    tail = jnp.where(u == 1.0, e, jnp.log(u) * e / jnp.where(u == 1.0, 1.0, u - 1.0))
    return jnp.maximum(v, 0.0) + tail


def lanes(sm, first, count):
    return jnp.concatenate(
        [sm[half, r : r + 1, :] for half in range(2) for r in range(first, first + count)],
        axis=1,
    )


def decay_weights(sm):
    rows = [lanes(sm, R_WD + 4 * i, 4) for i in range(8)]
    rows.append(jnp.zeros((TOK - 8, WIDTH), F32))
    return jnp.concatenate(rows, axis=0).astype(BF16)


def layout(lens, owner, replica):
    i, j = iota(0), iota(1)
    owned = (owner == replica).astype(F32)
    held = lens.astype(F32) * owned
    ends = jnp.sum(jnp.where(j <= i, held, 0.0), axis=1, keepdims=True)
    owned_col = jnp.sum(jnp.where(j == i, owned, 0.0), axis=1, keepdims=True)
    done = jnp.where(ends <= j.astype(F32), owned_col, 0.0)
    seg_row = jnp.sum(done, axis=0, keepdims=True)
    seg_col = jnp.sum(jnp.where(j == i, seg_row, 0.0), axis=1, keepdims=True)
    total = jnp.sum(held, axis=1, keepdims=True)
    t = iota(0, (TOK, 1)).astype(F32)
    usable = (t < total).astype(F32)
    return seg_col, seg_row, usable


def links(seg_col):
    wide = jnp.broadcast_to(seg_col, (TOK, TOK))
    t = iota(0)
    return [
        ((pltpu.roll(wide, d, 0) == wide) & (t >= d)).astype(F32)[:, :1] for d in range(1, TAPS)
    ]


def conv_tile(sig, taps_rows, link):
    out = sig * taps_rows[TAPS - 1]
    for d in range(1, TAPS):
        out = out + pltpu.roll(sig, d, 0) * link[d - 1] * taps_rows[TAPS - 1 - d]
    return out


def norm_rows(v):
    return lax.rsqrt(jnp.mean(v * v, axis=-1, keepdims=True) + EPS)


def decays(dec, sm):
    alog = sm[0, R_ALOG : R_ALOG + 1, :] + sm[1, R_ALOG : R_ALOG + 1, :]
    bias = sm[0, R_BIAS : R_BIAS + 1, :] + sm[1, R_BIAS : R_BIAS + 1, :]
    z = dec + bias
    rate = -jnp.exp(alog)
    logdecay = rate * softplus(z)
    tri = (iota(1) <= iota(0)).astype(F32)
    summed = nn(tri, logdecay, HI)
    return z, rate, logdecay, summed, sigmoid(dec)


def inverse(systems):
    i, j = iota(0), iota(1)
    eye = (i == j).astype(F32)
    low = i > j
    found = [eye - jnp.where(low & ((i // 2) == (j // 2)), a, 0.0) for a in systems]
    size = 2
    while size < TOK:
        mask = low & ((i // (2 * size)) == (j // (2 * size))) & ((i // size) != (j // size))
        inner = [nn(jnp.where(mask, a, 0.0), m, M_INV) for a, m in zip(systems, found)]
        found = [m - nn(m, b, M_INV) for m, b in zip(found, inner)]
        size *= 2
    return found


def head_inputs(proj, taps, link, h):
    out = []
    for first, width in (
        (KEY_DIM * h, KEY_DIM),
        (HEADS * KEY_DIM + KEY_DIM * h, KEY_DIM),
        (2 * HEADS * KEY_DIM + VALUE_DIM * h, VALUE_DIM),
    ):
        rows = [t[:, first : first + width] for t in taps]
        out.append((first, width, rows, conv_tile(proj[:, first : first + width], rows, link)))
    return out


WEIGHT_SHAPES = ((WIDTH, PROJ), (WIDTH, WIDTH), (WIDTH, 2 * HIDDEN_FF), (HIDDEN_FF, WIDTH))


def forward_body(
    x_ref, sm_ref, rows_of, out_ref, proj_ref, dec_ref, inv_ref, mid_ref, gu_ref,
    w_in, w_out, w_ff, w_down, mixed_ref, hid_ref, hook,
):
    seg_col, seg_row, _ = rows_of
    link = links(seg_col)
    same = (seg_col == seg_row).astype(F32)
    xf = x_ref[...].astype(F32)
    normed = (xf * norm_rows(xf) * lanes(sm_ref, R_GIN, 4)).astype(BF16)
    dec = nt(normed, decay_weights(sm_ref))
    dec_ref[...] = dec
    hook("in")

    @pl.loop(0, PROJ // 512)
    def _(c):
        cols = pl.ds(pl.multiple_of(c * 512, 512), 512)
        proj_ref[:, cols] = nn(normed, w_in[:, cols])

    z, rate, logdecay, summed, beta = decays(dec, sm_ref)
    summed_t = summed.T
    taps = [lanes(sm_ref, R_TAPS + 8 * k, 8) for k in range(TAPS)]
    i, j = iota(0), iota(1)
    strict = i > j
    kept, systems = [], []
    for h in range(HEADS):
        (_, _, _, qc), (_, _, _, kc), (_, _, _, vc) = head_inputs(proj_ref, taps, link, h)
        q, k, v = (c * sigmoid(c) for c in (qc, kc, vc))
        q = q * lax.rsqrt(jnp.sum(q * q, axis=-1, keepdims=True) + EPS) * KEY_DIM ** (-0.5)
        k = k * lax.rsqrt(jnp.sum(k * k, axis=-1, keepdims=True) + EPS)
        w = jnp.exp(jnp.minimum(summed[:, h : h + 1] - summed_t[h : h + 1, :], 0.0)) * same
        b = beta[:, HEADS + h : HEADS + h + 1]
        gram = nt(k, k, M_FWD)
        systems.append(jnp.where(strict, b * gram * w, 0.0))
        scores = jnp.where(i >= j, nt(q, k, M_FWD) * w, 0.0)
        kept.append((scores, b * v))
        hook(h)
    inv = inverse(systems)
    hook("inverse")
    gain_out = lanes(sm_ref, R_GOUT, 1)
    for h in range(HEADS):
        inv_ref[h] = inv[h]
        scores, bv = kept[h]
        delta = nn(scores, nn(inv[h], bv, M_FWD), M_FWD)
        cols = slice(VALUE_DIM * h, VALUE_DIM * (h + 1))
        gate = proj_ref[:, CONV + VALUE_DIM * h : CONV + VALUE_DIM * (h + 1)]
        mixed_ref[:, cols] = (
            delta * norm_rows(delta) * gain_out * (gate * sigmoid(gate))
        ).astype(BF16)
    hook("out")
    mid = xf + nn(mixed_ref[...], w_out[...])
    mid_ref[...] = mid
    normed_ff = (mid * norm_rows(mid) * lanes(sm_ref, R_GFF, 4)).astype(BF16)
    hook("ff")

    @pl.loop(0, HIDDEN_FF // 128)
    def _(c):
        a = pl.ds(pl.multiple_of(c * 128, 128), 128)
        b = pl.ds(pl.multiple_of(HIDDEN_FF + c * 128, 128), 128)
        gate = nn(normed_ff, w_ff[:, a])
        up = nn(normed_ff, w_ff[:, b])
        gu_ref[:, a] = gate
        gu_ref[:, b] = up
        hid_ref[:, a] = (gate * sigmoid(gate) * up).astype(BF16)

    hook("down")
    out_ref[...] = (mid + nn(hid_ref[...], w_down[...])).astype(BF16)


def backward_body(
    x_ref, cot_ref, sm_ref, rows_of,
    proj_ref, dec_ref, inv_ref, mid_ref, gu_ref,
    dx_ref, small_ref, nrm_t, mix_t, nff_t, hid_t, dproj_ref, dmid_ref, dgu_ref, dout_ref,
    w_in, w_out, w_ff, w_down, dmix_ref, hook,
):
    i, j = iota(0), iota(1)
    seg_col, seg_row, _ = rows_of
    link = links(seg_col)
    same = (seg_col == seg_row).astype(F32)
    dout = cot_ref[...].astype(F32)
    doutb = dout.astype(BF16)
    dout_ref[...] = doutb
    small_ref[...] = jnp.zeros_like(small_ref)

    for c in range(HIDDEN_FF // 128):
        a = slice(c * 128, c * 128 + 128)
        b = slice(HIDDEN_FF + c * 128, HIDDEN_FF + c * 128 + 128)
        gate, up = gu_ref[:, a], gu_ref[:, b]
        sg = sigmoid(gate)
        d_hidden = nt(doutb, w_down[a, :])
        dgu_ref[:, a] = (d_hidden * up * sg * (1.0 + gate * (1.0 - sg))).astype(BF16)
        dgu_ref[:, b] = (d_hidden * gate * sg).astype(BF16)
        hid_t[a, :] = (gate * sg * up).T.astype(BF16)
    mid = mid_ref[...]
    r = norm_rows(mid)
    n = mid * r
    gain_ff = lanes(sm_ref, R_GFF, 4)
    nff_t[...] = (n * gain_ff).T.astype(BF16)
    hook("ff")

    @pl.loop(0, WIDTH // 256)
    def _(c):
        rows = pl.ds(pl.multiple_of(c * 256, 256), 256)
        dmix_ref[:, rows] = nt(dgu_ref[...], w_ff[rows, :])

    d = dmix_ref[...]
    put(small_ref, R_GFF, 4, jnp.sum(d * n, axis=0, keepdims=True))
    d = d * gain_ff
    dmid = dout + r * (d - n * jnp.mean(d * n, axis=-1, keepdims=True))
    dmidb = dmid.astype(BF16)
    dmid_ref[...] = dmidb
    dmix_ref[...] = nt(dmidb, w_out[...])

    z, rate, logdecay, summed, beta = decays(dec_ref[...], sm_ref)
    summed_t = summed.T
    taps = [lanes(sm_ref, R_TAPS + 8 * k, 8) for k in range(TAPS)]
    gain_out = lanes(sm_ref, R_GOUT, 1)
    strict, causal = i > j, i >= j
    d_gain_out = jnp.zeros((1, VALUE_DIM), F32)
    d_col = jnp.zeros((TOK, TOK), F32)
    d_row = jnp.zeros((TOK, TOK), F32)
    for h in range(HEADS):
        parts = head_inputs(proj_ref, taps, link, h)
        sig = [sigmoid(p[3]) for p in parts]
        qa, ka, v = (p[3] * s for p, s in zip(parts, sig))
        rq = lax.rsqrt(jnp.sum(qa * qa, axis=-1, keepdims=True) + EPS)
        rk = lax.rsqrt(jnp.sum(ka * ka, axis=-1, keepdims=True) + EPS)
        q = qa * rq * KEY_DIM ** (-0.5)
        k = ka * rk
        w = jnp.exp(jnp.minimum(summed[:, h : h + 1] - summed_t[h : h + 1, :], 0.0)) * same
        b = beta[:, HEADS + h : HEADS + h + 1]
        gram = nt(k, k, M_FWD)
        qk = nt(q, k, M_FWD)
        ws = jnp.where(strict, w, 0.0)
        wc = jnp.where(causal, w, 0.0)
        scores = qk * wc
        inv = inv_ref[h]
        u = nn(inv, b * v, M_FWD)
        delta = nn(scores, u, M_FWD)
        gcols = slice(CONV + VALUE_DIM * h, CONV + VALUE_DIM * (h + 1))
        vcols = slice(VALUE_DIM * h, VALUE_DIM * (h + 1))
        gate = proj_ref[:, gcols]
        sg = sigmoid(gate)
        si = gate * sg
        rd = norm_rows(delta)
        nd = delta * rd
        dm = dmix_ref[:, vcols]
        mix_t[vcols, :] = (nd * gain_out * si).T.astype(BF16)
        dproj_ref[:, gcols] = (dm * nd * gain_out * sg * (1.0 + gate * (1.0 - sg))).astype(BF16)
        dn = dm * si
        d_gain_out = d_gain_out + jnp.sum(dn * nd, axis=0, keepdims=True)
        dn = dn * gain_out
        ddelta = rd * (dn - nd * jnp.mean(dn * nd, axis=-1, keepdims=True))
        dscores = nt(ddelta, u, 3)
        du = tn(scores, ddelta, 3)
        dr = tn(inv, du, 3)
        da = -nt(dr, u, 3)
        dqk = dscores * wc
        dgram = da * b * ws
        pair = dqk * qk + dgram * gram
        dq = nn(dqk, k, M_BWD)
        dk = tn(dqk, q, M_BWD) + nn(dgram + dgram.T, k, M_BWD)
        dv = b * dr
        dbeta = jnp.sum(da * gram * ws, axis=1, keepdims=True) + jnp.sum(
            dr * v, axis=1, keepdims=True
        )
        d_col = jnp.where(j == h, jnp.sum(pair, axis=1, keepdims=True), d_col)
        d_col = jnp.where(j == HEADS + h, dbeta, d_col)
        d_row = jnp.where(i == h, jnp.sum(pair, axis=0, keepdims=True), d_row)
        dq = KEY_DIM ** (-0.5) * dq
        dqa = rq * dq - qa * (rq * rq * rq) * jnp.sum(dq * qa, axis=-1, keepdims=True)
        dka = rk * dk - ka * (rk * rk * rk) * jnp.sum(dk * ka, axis=-1, keepdims=True)
        for (first, width, rows, c), s, dact in zip(parts, sig, (dqa, dka, dv)):
            dc = dact * s * (1.0 + c * (1.0 - s))
            raw = proj_ref[:, first : first + width]
            total = dc * rows[TAPS - 1]
            put_taps(small_ref, TAPS - 1, first, jnp.sum(dc * raw, axis=0, keepdims=True))
            for dist in range(1, TAPS):
                dcl = dc * link[dist - 1]
                put_taps(
                    small_ref, TAPS - 1 - dist, first,
                    jnp.sum(dcl * pltpu.roll(raw, dist, 0), axis=0, keepdims=True),
                )
                total = total + pltpu.roll(dcl, TOK - dist, 0) * rows[TAPS - 1 - dist]
            dproj_ref[:, first : first + width] = total.astype(BF16)
        hook(h)
    put(small_ref, R_GOUT, 1, d_gain_out)
    d_summed = d_col - d_row.T
    later = (j >= i).astype(F32)
    dlog = nn(later, d_summed, HI)
    dz = dlog * rate * sigmoid(z)
    head_lane = j < HEADS
    d_alog = jnp.sum(jnp.where(head_lane, dlog * logdecay, 0.0), axis=0, keepdims=True)
    d_bias = jnp.sum(jnp.where(head_lane, dz, 0.0), axis=0, keepdims=True)
    for half in range(2):
        small_ref[half, R_ALOG : R_ALOG + 1, :] = d_alog
        small_ref[half, R_BIAS : R_BIAS + 1, :] = d_bias
    ddec = jnp.where(
        head_lane, dz, jnp.where(j < 2 * HEADS, d_col * beta * (1.0 - beta), 0.0)
    ).astype(BF16)

    xf = x_ref[...].astype(F32)
    r = norm_rows(xf)
    n = xf * r
    gain_in = lanes(sm_ref, R_GIN, 4)
    normed = (n * gain_in).astype(BF16)
    nrm_t[...] = (n * gain_in).T.astype(BF16)
    hook("mixer")
    gwd = tn(ddec, normed)
    for row in range(2 * HEADS):
        put(small_ref, R_WD + 4 * row, 4, gwd[row : row + 1, :])

    @pl.loop(0, WIDTH // 256)
    def _(c):
        rows = pl.ds(pl.multiple_of(c * 256, 256), 256)
        dmix_ref[:, rows] = nt(dproj_ref[...], w_in[rows, :])

    d = dmix_ref[...] + nn(ddec, decay_weights(sm_ref))
    put(small_ref, R_GIN, 4, jnp.sum(d * n, axis=0, keepdims=True))
    d = d * gain_in
    dx_ref[...] = (dmid + r * (d - n * jnp.mean(d * n, axis=-1, keepdims=True))).astype(BF16)


def put(ref, first, count, row):
    for half in range(2):
        for c in range(count):
            at = (half * count + c) * 128
            ref[half, first + c : first + c + 1, :] = row[:, at : at + 128]


def put_taps(ref, tap, first, row):
    for c in range(row.shape[1] // 128):
        block = first // 128 + c
        at = R_TAPS + 8 * tap + block % 8
        ref[block // 8, at : at + 1, :] = row[:, c * 128 : c * 128 + 128]


ORDERS = ((0, 1, 2, 3), (1, 0, 3, 2), (2, 3, 0, 1), (3, 2, 1, 0))
FLAT = (
    (2, 0, 256, 1, False),
    (2, 256, 768, 3, True),
    (2, 1024, 768, 2, False),
    (2, 1792, 1024, 1, True),
    (3, 0, 1024, 0, False),
    (0, 0, 1024, 3, False),
    (0, 1024, 1024, 1, False),
    (0, 2048, 768, 2, False),
    (0, 2816, 256, 2, False),
    (1, 0, 512, 0, True),
    (1, 512, 512, 2, True),
)
ORDER = (
    (5, 0), (6, 0), (7, 0), (8, 0), (9, 0), (10, 0), (0, 1), (11, 0), (1, 1), (2, 1), (11, 1),
    (5, 1), (4, 1), (6, 1), (7, 1), (0, 2), (3, 1), (1, 2), (8, 1), (11, 2), (2, 2), (9, 1),
    (6, 2), (5, 2), (4, 2), (2, 3), (7, 2), (1, 3), (0, 3), (10, 1), (8, 2), (9, 2), (3, 2),
    (4, 3), (0, 4), (7, 3), (6, 3), (8, 3), (0, 5), (10, 2), (4, 4), (5, 3), (3, 3), (6, 4),
    (0, 6), (11, 3), (2, 4), (1, 4), (10, 3), (4, 5), (6, 5), (5, 4), (2, 5), (9, 3), (3, 4),
    (0, 7), (1, 5), (7, 4), (8, 4), (10, 4), (4, 6), (6, 6), (5, 5), (2, 6), (9, 4), (0, 8),
    (7, 5), (3, 5), (8, 5), (10, 5), (1, 6), (11, 4), (5, 6), (6, 7), (4, 7), (9, 5), (2, 7),
    (0, 9), (3, 6), (7, 6), (8, 6), (10, 6), (9, 6), (1, 7), (5, 7), (6, 8), (2, 8), (9, 7),
    (11, 5), (7, 7), (8, 7), (3, 7), (10, 7), (1, 8), (4, 8), (7, 8), (5, 8), (8, 8), (3, 8),
    (10, 8), (6, 9), (2, 9), (9, 8), (1, 9), (4, 9), (7, 9), (8, 9), (3, 9), (9, 9), (5, 9),
    (10, 9),
)

GATHER = (
    (2, 0, 768, 0, True), (2, 768, 768, 1, True), (2, 1536, 768, 3, True), (2, 2304, 512, 2, True),
    (3, 0, 1024, 2, False), (0, 0, 1024, 0, False), (0, 1024, 1024, 1, False),
    (0, 2048, 1024, 3, False), (1, 0, 256, 0, False), (1, 256, 512, 1, False),
    (1, 768, 256, 3, False),
)
DOWN = 3


class Place:
    def __init__(self):
        self.section = lax.axis_index("section")
        dp = lax.axis_index("dp")
        self.half = lax.axis_index("fsdp")
        x, z, core = dp // 8, (dp // 2) % 4, dp % 2
        self.core = core

        def at(x, z, core, half):
            return (self.section, (x * 4 + z) * 2 + core, half)

        xa, za = x + 1 - 2 * (x % 2), z + 1 - 2 * (z % 2)
        self.links = (
            at(xa, z, core, self.half),
            at(3 - x, z, core, self.half),
            at(x, za, core, self.half),
            at(x, 3 - z, core, self.half),
        )
        self.sibling = at(x, z, 1 - core, self.half)
        self.pair = at(x, z, core, 1 - self.half)
        self.other = (1 - self.section, dp, self.half)
        self.bits = ((x % 2 + x // 2) % 2, x // 2, (z % 2 + z // 2) % 2, z // 2)

    def greet(self, *more):
        barrier = pltpu.get_barrier_semaphore()
        everyone = (*self.links, self.sibling, self.pair, *more)
        for device in everyone:
            pl.semaphore_signal(
                barrier, inc=1, device_id=device, device_id_type=pl.DeviceIdType.MESH
            )
        pl.semaphore_wait(barrier, len(everyone))


class Chunk:
    def __init__(self, place, weight, first, width, flavor, pair_first=False):
        self.pair_first = pair_first
        self.weight, self.first, self.width, self.order = weight, first, width, ORDERS[flavor]
        self.bits = [place.bits[d] for d in self.order]
        self.partners = [place.links[d] for d in self.order]
        self.rows = 352 if weight == DOWN else 256

    def size(self, steps):
        if self.weight == DOWN:
            return (self.rows >> min(steps, 1), self.width >> max(steps - 1, 0))
        return (self.rows >> steps, self.width)

    def start(self, steps, other=False):
        row = col = 0
        for k in range(1, steps + 1):
            bit = self.bits[k - 1]
            if other and k == steps:
                bit = 1 - bit
            if self.weight == DOWN and k > 1:
                col = col + bit * self.size(k)[1]
            else:
                row = row + bit * self.size(k)[0]
        return row, col

    def window(self, steps, other=False, row0=0, col0=0):
        (row, col), (rows, cols) = self.start(steps, other), self.size(steps)
        row, col = row + row0, col + col0
        if not isinstance(row, int):
            row = pl.multiple_of(row, 16)
        if not isinstance(col, int):
            col = pl.multiple_of(col, 128)
        return pl.ds(row, rows), pl.ds(col, cols)


def send(src, dst, sems, k, device):
    copy = pltpu.make_async_remote_copy(
        src_ref=src, dst_ref=dst, send_sem=sems[0].at[k], recv_sem=sems[1].at[k],
        device_id=device, device_id_type=pl.DeviceIdType.MESH,
    )
    copy.start()
    return copy


HALF_ROWS = (512, 512, 512, 704)
COLUMNS = (PROJ, WIDTH, 2 * HIDDEN_FF, WIDTH)


GATHER_FLAT = tuple(
    c[:4] for c in sorted(GATHER, key=lambda c: (0, 3, 1, 2)[c[0]])
)
PACKED = 0
STAGES = 6


def layers_kernel(
    x_ref, cot_ref, mask_ref, lens_ref, own_ref,
    gin_ref, gff_ref, gout_ref, taps_ref, wdec_ref, alog_ref, bias_ref, wi, wo, wf, wd,
    out_ref, dx_ref, tot_ref, g_in, g_out, g_ff, g_down,
    small_ref, nrm_t, mix_t, nff_t, hid_t, dproj_ref, dmid_ref, dgu_ref, dout_ref,
    w_in, w_out, w_ff, w_down, sm_ref, pk_wide, pk_ref, pk_far, proj_ref, dec_ref, inv_ref,
    mid_ref, gu_ref, mixed_ref, hid_ref, dmix_ref, xin_ref, next_ref, cin_ref, back_ref,
    send_sem, recv_sem, local_sem, *scratch,
):
    place = Place()
    pk_wide[...] = jnp.zeros_like(pk_wide)
    for ref, first, per_row in (
        (gin_ref, R_GIN, 4), (gff_ref, R_GFF, 4), (gout_ref, R_GOUT, 1), (taps_ref, R_TAPS, 8),
        (wdec_ref, R_WD, 4),
    ):
        rows = ref[...].astype(F32)
        for r in range(rows.shape[0]):
            for c in range(per_row):
                at = first + r * per_row + c
                pk_wide[at : at + 1, :] = rows[r : r + 1, c * 128 : c * 128 + 128]
    for ref, at in ((alog_ref, R_ALOG), (bias_ref, R_BIAS)):
        two = ref[...].astype(F32)
        none = jnp.zeros((1, 2), F32)
        pk_wide[at : at + 1, 0:2] = jnp.where(place.half == 0, two, none)
        pk_wide[at : at + 1, 2:4] = jnp.where(place.half == 0, none, two)
    pk_ref[...] = pk_wide[...].astype(BF16)
    sems = (send_sem, recv_sem)
    shards, whole = (wi, wo, wf, wd), (w_in, w_out, w_ff, w_down)
    chunks = [Chunk(place, *c) for c in GATHER_FLAT]
    count = len(chunks)
    first = {w: [n for n, c in enumerate(chunks) if c.weight == w] for w in range(4)}

    def make(src, dst, k, device):
        return pltpu.make_async_remote_copy(
            src_ref=src, dst_ref=dst, send_sem=sems[0].at[k], recv_sem=sems[1].at[k],
            device_id=device, device_id_type=pl.DeviceIdType.MESH,
        )

    def local(w):
        rows = HALF_ROWS[w]
        at = pl.ds(pl.multiple_of(place.half * rows, 16), rows)
        return pltpu.make_async_copy(shards[w], whole[w].at[at, :], local_sem.at[w])

    def stage_copy(n, stage):
        c = chunks[n]
        w, rows = c.weight, HALF_ROWS[c.weight]
        k = 1 + stage * count + n
        if stage == 0:
            src = shards[w].at[c.window(4, row0=place.core * c.rows, col0=c.first)]
            to = c.window(4, row0=place.half * rows + place.core * c.rows, col0=c.first)
            return make(src, whole[w].at[to], k, place.pair)
        row0 = (1 - place.half) * rows + place.core * c.rows
        block = whole[w].at[c.window(5 - stage, row0=row0, col0=c.first)]
        device = c.partners[4 - stage] if stage < 5 else place.sibling
        return make(block, block, k, device)

    def passed_on(ns, stage):
        for n in ns:
            stage_copy(n, stage - 1).wait_recv()
            stage_copy(n, stage).start()

    rest = first[1] + first[2] + first[3]

    def complete(w):
        for n in first[w]:
            stage_copy(n, STAGES - 1).wait_recv()
        local(w).wait()

    def gather_hook(point):
        if point == "in":
            for stage in range(1, 4):
                passed_on(first[0], stage)
                if stage == 1:
                    passed_on(rest, 1)
            passed_on(first[0], 4)
            passed_on(rest, 2)
            passed_on(first[0], 5)
            complete(0)
        elif point == 0:
            passed_on(rest, 3)
        elif point == 2:
            passed_on(rest, 4)
        elif point == "inverse":
            passed_on(rest, 5)
        elif point in ("out", "ff", "down"):
            complete({"out": 1, "ff": 2, "down": 3}[point])

    place.greet(place.other)
    packed = make(pk_ref, pk_far, PACKED, place.pair)
    packed.start()
    for w in (0, 1, 2, 3):
        for n in first[w]:
            stage_copy(n, 0).start()
        local(w).start()
    rows_of = layout(lens_ref[...], own_ref[...], lax.axis_index("dp") * 2 + place.half)
    packed.wait()
    sm_ref[place.half] = pk_ref[...].astype(F32)
    sm_ref[1 - place.half] = pk_far[...].astype(F32)
    xin_ref[...] = x_ref[...]
    forth = make(out_ref, next_ref, 1 + STAGES * count, place.other)
    back = make(dx_ref, back_ref, 2 + STAGES * count, place.other)
    section = place.section

    @pl.loop(0, 2)
    def _(turn):
        def hook(point):
            @pl.when(turn == 0)
            def _():
                gather_hook(point)

        forward_body(
            xin_ref, sm_ref, rows_of, out_ref, proj_ref, dec_ref, inv_ref, mid_ref, gu_ref,
            w_in, w_out, w_ff, w_down, mixed_ref, hid_ref, hook,
        )

        @pl.when(turn == 0)
        def _():
            forth.start()
            forth.wait()
            xin_ref[...] = jnp.where(section == 0, x_ref[...], next_ref[...])

    mask = jnp.sum(
        jnp.where(iota(0) == iota(1), mask_ref[...].astype(F32), 0.0), axis=1, keepdims=True
    )
    cin_ref[...] = (cot_ref[...].astype(F32) * (mask * rows_of[2])).astype(BF16)

    cross, event, small_step, close, sums = reducer(
        place, (nrm_t, mix_t, nff_t, hid_t), (dproj_ref, dmid_ref, dgu_ref, dout_ref),
        (g_in, g_out, g_ff, g_down), scratch,
    )

    def reduce_hook(point):
        if point == "ff":
            cross(2)
            cross(3)
        elif point == 0:
            event(0, 0)
            event(1, 0)
        elif point == 1:
            event(2, 0)
            event(3, 0)
        elif point == 2:
            event(4, 0)
        elif point == "mixer":
            cross(0)
            cross(1)

    for turn in range(2):
        backward_body(
            xin_ref, cin_ref, sm_ref, rows_of,
            proj_ref, dec_ref, inv_ref, mid_ref, gu_ref,
            dx_ref, small_ref, nrm_t, mix_t, nff_t, hid_t, dproj_ref, dmid_ref, dgu_ref, dout_ref,
            w_in, w_out, w_ff, w_down, dmix_ref, reduce_hook if turn else (lambda point: None),
        )
        if turn == 0:
            back.start()
            back.wait()
            cin_ref[...] = jnp.where(section == 0, back_ref[...], cin_ref[...])

    sums[0] = small_ref[...]
    for n, stage in ORDER:
        if n == len(FLAT):
            small_step()
        else:
            event(n, stage)
    close(tot_ref)
    for n in range(count):
        for stage in range(STAGES):
            stage_copy(n, stage).wait_send()


def layers(x, cot, mask, lens, own, smalls, weights):
    vm = pl.BlockSpec(memory_space=pltpu.VMEM)
    hbm = pl.BlockSpec(memory_space=pl.ANY)
    tokens = (TOK, WIDTH)
    outs = [(tokens, BF16), (tokens, BF16), ((PACK, 128), F32)]
    outs += [((r, c), BF16) for r, c in zip(HALF_ROWS, COLUMNS)]
    scratch = [
        ((2, PACK, 128), F32), ((WIDTH, TOK), BF16), ((WIDTH, TOK), BF16), ((WIDTH, TOK), BF16),
        ((HIDDEN_FF, TOK), BF16), ((TOK, PROJ), BF16), (tokens, BF16),
        ((TOK, 2 * HIDDEN_FF), BF16), (tokens, BF16),
    ]
    scratch += [(s, BF16) for s in WEIGHT_SHAPES] + [
        ((2, PACK, 128), F32), ((PACK, 128), F32), ((PACK, 128), BF16), ((PACK, 128), BF16),
        ((TOK, PROJ), F32), ((TOK, TOK), F32), ((HEADS, TOK, TOK), F32), (tokens, F32),
        ((TOK, 2 * HIDDEN_FF), F32), (tokens, BF16), ((TOK, HIDDEN_FF), BF16), (tokens, F32),
        (tokens, BF16), (tokens, BF16), (tokens, BF16), (tokens, BF16),
    ]
    count = 3 + STAGES * len(GATHER_FLAT)
    return pl.pallas_call(
        layers_kernel,
        name="layers_and_sums",
        out_shape=[jax.ShapeDtypeStruct(s, d) for s, d in outs],
        in_specs=[vm] * 12 + [hbm] * 4,
        out_specs=[vm] * 3 + [hbm] * 4,
        scratch_shapes=[pltpu.VMEM(s, d) for s, d in scratch]
        + [
            pltpu.SemaphoreType.DMA((count,)),
            pltpu.SemaphoreType.DMA((count,)),
            pltpu.SemaphoreType.DMA((4,)),
        ]
        + reducer_scratch(),
        compiler_params=pltpu.CompilerParams(
            collective_id=1, has_side_effects=True, vmem_limit_bytes=VMEM_LIMIT
        ),
    )(x, cot, mask, lens, own, *smalls, *weights)


def reducer(place, lhs, rhs, grads, scratch):
    peer_l, peer_r = scratch[0:4], scratch[4:8]
    count = len(FLAT)
    parts, fins = scratch[8 : 8 + count], scratch[8 + count : 8 + 2 * count]
    scratch = scratch[8 + 2 * count :]
    arrived = [scratch[5 * n : 5 * n + 5] for n in range(count)]
    sums, sums_in, sums_pair, send_sem, recv_sem, local_sem = scratch[5 * count :]
    sems = (send_sem, recv_sem)
    ids = iter(range(10 * count + 18))
    chunks = [Chunk(place, *c) for c in FLAT]
    last, local, sent = {}, {}, []
    crossing = {}

    def cross(w):
        rows = peer_l[w].shape[1]
        found = []
        for h in range(2):
            at = pl.multiple_of(HALF_ROWS[w] * h + (1 - place.core) * rows, 16)
            found.append(
                send(lhs[w].at[pl.ds(at, rows), :], peer_l[w].at[h], sems, next(ids), place.sibling)
            )
        found.append(send(rhs[w], peer_r[w], sems, next(ids), place.sibling))
        sent.extend(found)
        crossing[w] = found


    def product(n, first):
        c = chunks[n]
        w = c.weight
        if c.pair_first:
            half = 1 - place.half if first else place.half
            blocks, rows = [(half, 0)], c.rows
        else:
            offset = pl.multiple_of(c.start(1, first)[0], 16)
            blocks, rows = [(0, offset), (1, offset)], c.size(1)[0]
        left = []
        for h, offset in blocks:
            at = pl.multiple_of(HALF_ROWS[w] * h + place.core * c.rows + offset, 16)
            left.append(
                jnp.concatenate(
                    [lhs[w][pl.ds(at, rows), :], peer_l[w][h, pl.ds(offset, rows), :]], axis=1
                )
            )
        both = left[0] if len(left) == 1 else jnp.concatenate(left, axis=0)
        for t in range(0, c.width, 256):
            cols = slice(c.first + t, c.first + t + 256)
            right = jnp.concatenate([rhs[w][:, cols], peer_r[w][:, cols]], axis=0)
            out = nn(both, right).astype(BF16)
            for k, (h, offset) in enumerate(blocks):
                parts[n][h, pl.ds(offset, rows), t : t + 256] = out[k * rows : (k + 1) * rows]

    def halves(n):
        return place.half if chunks[n].pair_first else slice(None)

    def give(n, step):
        c = chunks[n]
        at = c.window(step, other=True)
        last[n] = send(
            parts[n].at[halves(n), at[0], at[1]], arrived[n][step - 1], sems, next(ids),
            c.partners[step - 1],
        )
        sent.append(last[n])

    def add(n, step):
        c = chunks[n]
        (row, col), (rows, cols) = c.start(step), c.size(step)
        col = pl.ds(pl.multiple_of(col, 128), cols) if c.weight == DOWN else slice(None)
        lead = (slice(None),) if not c.pair_first else ()

        @pl.loop(0, rows // 16)
        def _(t):
            at = pl.ds(pl.multiple_of(row + t * 16, 16), 16)
            got = arrived[n][step - 1][(*lead, pl.ds(pl.multiple_of(t * 16, 16), 16), slice(None))]
            old = parts[n][halves(n), at, col]
            parts[n][halves(n), at, col] = (old.astype(F32) + got.astype(F32)).astype(BF16)

    def finish(n, block):
        c = chunks[n]
        fins[n][...] = block
        to = grads[c.weight].at[c.window(4, row0=place.core * c.rows, col0=c.first)]
        local[n] = pltpu.make_async_copy(fins[n], to, local_sem.at[n])
        local[n].start()
        last[n] = send(fins[n], to, sems, next(ids), c.partners[3])
        sent.append(last[n])

    def to_pair(n, src, dst):
        last[n] = send(src, dst, sems, next(ids), place.pair)
        sent.append(last[n])

    def event(n, stage):
        c = chunks[n]
        w = c.weight
        if stage == 0:
            for copy in crossing.pop(w, ()):
                copy.wait_recv()
            product(n, True)
            if c.pair_first:
                to_pair(n, parts[n].at[1 - place.half], arrived[n][4])
            else:
                give(n, 1)
            product(n, False)
        elif c.pair_first and stage == 1:
            last[n].wait_recv()

            @pl.loop(0, c.rows // 16)
            def _(t):
                at = pl.ds(pl.multiple_of(t * 16, 16), 16)
                old = parts[n][place.half, at, :].astype(F32)
                parts[n][place.half, at, :] = (old + arrived[n][4][at, :].astype(F32)).astype(BF16)

            give(n, 1)
        elif c.pair_first and stage <= 4:
            last[n].wait_recv()
            add(n, stage - 1)
            give(n, stage)
        elif c.pair_first and stage == 5:
            last[n].wait_recv()
            at = c.window(4)
            finish(
                n,
                (
                    parts[n][place.half, at[0], at[1]].astype(F32)
                    + arrived[n][3][...].astype(F32)
                ).astype(BF16),
            )
        elif stage <= 3:
            last[n].wait_recv()
            add(n, stage)
            give(n, stage + 1)
        elif stage == 4:
            last[n].wait_recv()
            add(n, 4)
            at = c.window(4)
            to_pair(n, parts[n].at[1 - place.half, at[0], at[1]], arrived[n][4])
        elif stage == 5:
            last[n].wait_recv()
            at = c.window(4)
            finish(
                n,
                (
                    parts[n][place.half, at[0], at[1]].astype(F32)
                    + arrived[n][4][...].astype(F32)
                ).astype(BF16),
            )
        elif stage <= 8:
            if stage == 6:
                local[n].wait()
            last[n].wait_recv()
            steps_left = 9 - stage
            block = grads[w].at[c.window(steps_left, row0=place.core * c.rows, col0=c.first)]
            last[n] = send(block, block, sems, next(ids), c.partners[steps_left - 1])
            sent.append(last[n])
        else:
            last[n].wait_recv()
            block = grads[w].at[c.window(0, row0=place.core * c.rows, col0=c.first)]
            last[n] = send(block, block, sems, next(ids), place.sibling)
            sent.append(last[n])

    small = []

    def small_step():
        steps = (place.sibling, *place.links)
        k = len(small)
        if 0 < k < 6:
            small[-1].wait_recv()
            sums[k] = sums[k - 1] + sums_in[k - 1]
        if k < 5:
            small.append(send(sums.at[k], sums_in.at[k], sems, next(ids), steps[k]))
        elif k == 5:
            small.append(
                send(sums.at[5, 1 - place.half], sums_pair, sems, next(ids), place.pair)
            )

    def close(tot_ref):
        while len(small) < 6:
            small_step()
        small[-1].wait_recv()
        tot_ref[...] = sums[5, place.half] + sums_pair[...]
        for n in range(count):
            last[n].wait_recv()
        for copy in sent + small:
            copy.wait_send()

    return cross, event, small_step, close, sums


class Sizes:
    bits = (0, 0, 0, 0)
    links = (None,) * 4


def reducer_scratch():
    chunks = [Chunk(Sizes, *c) for c in FLAT]
    count = len(FLAT)
    scratch = [pltpu.VMEM((2, r // 2, TOK), BF16) for r in HALF_ROWS]
    scratch += [pltpu.VMEM((TOK, c), BF16) for c in COLUMNS]
    scratch += [pltpu.VMEM((2, *c.size(0)), BF16) for c in chunks]
    scratch += [pltpu.VMEM(c.size(4), BF16) for c in chunks]
    for c in chunks:
        lead = () if c.pair_first else (2,)
        scratch += [pltpu.VMEM((*lead, *c.size(k)), BF16) for k in range(1, 5)]
        scratch.append(pltpu.VMEM(c.size(0 if c.pair_first else 4), BF16))
    total = 10 * count + 18
    scratch += [
        pltpu.VMEM((6, 2, PACK, 128), F32),
        pltpu.VMEM((5, 2, PACK, 128), F32),
        pltpu.VMEM((PACK, 128), F32),
        pltpu.SemaphoreType.DMA((total,)),
        pltpu.SemaphoreType.DMA((total,)),
        pltpu.SemaphoreType.DMA((count,)),
    ]
    return scratch


def finish_kernel(tot_ref, out_ref, dx_ref, *refs):
    sources, (o_gin, o_taps, o_wd, o_alog, o_bias, o_gout, o_gff) = refs[:4], refs[4:11]
    targets, o_out, o_dx = refs[11:15], refs[15], refs[16]
    narrow, wide = refs[17:21], refs[21:25]
    t_out, t_dx, in_sem, out_sem = refs[25:]
    half = lax.axis_index("fsdp")
    blocks = []
    for w, rows in enumerate(HALF_ROWS):
        size = rows // 4
        blocks += [(w, slice(k * size, (k + 1) * size)) for k in range(4)]
    loads = [
        pltpu.make_async_copy(sources[w].at[at], narrow[w].at[at], in_sem.at[k])
        for k, (w, at) in enumerate(blocks)
    ]
    for copy in loads:
        copy.start()
    tokens = ((out_ref, t_out, o_out), (dx_ref, t_dx, o_dx))
    passing = [
        pltpu.make_async_copy(src, via, in_sem.at[16 + k]) for k, (src, via, _) in enumerate(tokens)
    ]
    for copy in passing:
        copy.start()

    def row(first, count):
        return jnp.concatenate([tot_ref[first + k : first + k + 1, :] for k in range(count)], 1)

    o_gin[...] = row(R_GIN, 4)
    o_gff[...] = row(R_GFF, 4)
    o_gout[...] = row(R_GOUT, 1)
    for k in range(TAPS):
        o_taps[k : k + 1, :] = row(R_TAPS + 8 * k, 8)
    for k in range(2 * HEADS):
        o_wd[k : k + 1, :] = row(R_WD + 4 * k, 4)
    for ref, at in ((o_alog, R_ALOG), (o_bias, R_BIAS)):
        both = row(at, 1)
        ref[...] = jnp.where(half == 0, both[:, 0:2], both[:, 2:4])
    stores = []
    for k, (_, via, dst) in enumerate(tokens):
        passing[k].wait()
        stores.append(pltpu.make_async_copy(via, dst, out_sem.at[16 + k]))
        stores[-1].start()
    for k, (w, at) in enumerate(blocks):
        loads[k].wait()
        first, count = at.start, at.stop - at.start

        @pl.loop(0, count // 16)
        def _(t):
            here = pl.ds(pl.multiple_of(first + t * 16, 16), 16)
            wide[w][here, :] = narrow[w][here, :].astype(F32)

        copy = pltpu.make_async_copy(wide[w].at[at], targets[w].at[at], out_sem.at[k])
        copy.start()
        stores.append(copy)
    for copy in stores:
        copy.wait()


def finished(total, out, dx, grads):
    vm = pl.BlockSpec(memory_space=pltpu.VMEM)
    hbm = pl.BlockSpec(memory_space=pl.ANY)
    small = [(1, 512), (TAPS, 1024), (2 * HEADS, 512), (1, 2), (1, 2), (1, 128), (1, 512)]
    shapes = list(zip(HALF_ROWS, COLUMNS))
    return pl.pallas_call(
        finish_kernel,
        name="widen_gradients",
        out_shape=[jax.ShapeDtypeStruct(s, F32) for s in small + shapes]
        + [jax.ShapeDtypeStruct((TOK, WIDTH), BF16)] * 2,
        in_specs=[vm] + [hbm] * 6,
        out_specs=[vm] * 7 + [hbm] * 6,
        scratch_shapes=[pltpu.VMEM(s, BF16) for s in shapes]
        + [pltpu.VMEM(s, F32) for s in shapes]
        + [pltpu.VMEM((TOK, WIDTH), BF16)] * 2
        + [pltpu.SemaphoreType.DMA((18,)), pltpu.SemaphoreType.DMA((18,))],
        compiler_params=pltpu.CompilerParams(vmem_limit_bytes=VMEM_LIMIT),
    )(total, out, dx, *grads)


def on_device(
    inputs, out_grad, doc_lengths, doc_owner, loss_mask, gain_in, w_in, taps, w_decay, a_log,
    dt_bias, gain_out, w_out, gain_ff, w_ff_in, w_down,
):
    lens, own, mask = (a.reshape(1, TOK) for a in (doc_lengths, doc_owner, loss_mask))
    smalls = (gain_in, gain_ff, gain_out, taps[0].T, w_decay[0].T, a_log, dt_bias)
    mine = (w_in[0], w_out[0], w_ff_in[0], w_down[0])
    out, dx, total, *grads = layers(inputs, out_grad, mask, lens, own, smalls, mine)
    gin, g_taps, g_wd, g_alog, g_bias, g_gout, g_gff, g_in, g_out, g_ff, g_down, out, dx = finished(
        total, out, dx, grads
    )
    return (
        out[None], dx[None], gin, g_in[None], g_taps.T[None], g_wd.T[None], g_alog, g_bias, g_gout,
        g_out[None], g_gff, g_ff[None], g_down[None],
    )


def solution(mesh):
    tokens, pair = P(("dp", "fsdp"), None), P("section", "fsdp")
    matrix = P("section", "fsdp", None)
    params = (pair, matrix, matrix, matrix, pair, pair, pair, matrix, pair, matrix, matrix)
    return jax.shard_map(
        on_device,
        mesh=mesh,
        in_specs=(tokens, tokens, P(), P(), P(("dp", "fsdp")), *params),
        out_specs=(P("section", ("dp", "fsdp"), None),) * 2 + params,
        check_vma=False,
    )
```

```python
import functools
import math

import jax
import jax.numpy as jnp
from jax import lax
from jax.experimental import pallas as pl
from jax.experimental.pallas import tpu as pltpu
from jax.sharding import PartitionSpec as P

WIDTH = 1024
HEADS = 4
KEY_DIM = 128
VALUE_DIM = 256
HIDDEN_FF = 1408
TAPS = 4
TOK = 128
PROJ = 3072
CONV = 2048
EPS = 1e-06
PACK = 80
F32 = jnp.float32
BF16 = jnp.bfloat16
HI = lax.Precision.HIGHEST
M_INV, M_FWD, M_BWD = 3, 3, None
VMEM_LIMIT = 58 * 1024 * 1024

R_GIN, R_GFF, R_GOUT, R_TAPS, R_WD, R_ALOG, R_BIAS = 0, 4, 8, 9, 41, 73, 74


def dot(a, b, dims, mode):
    if mode != 3:
        if mode is None:
            a, b = a.astype(BF16), b.astype(BF16)
        return lax.dot_general(a, b, dims, precision=mode, preferred_element_type=F32)
    a1, b1 = a.astype(BF16), b.astype(BF16)
    a2, b2 = (a - a1.astype(F32)).astype(BF16), (b - b1.astype(F32)).astype(BF16)
    one = functools.partial(lax.dot_general, dimension_numbers=dims, preferred_element_type=F32)
    return one(a1, b1) + (one(a1, b2) + one(a2, b1))


def nn(a, b, mode=None):
    return dot(a, b, (((1,), (0,)), ((), ())), mode)


def nt(a, b, mode=None):
    return dot(a, b, (((1,), (1,)), ((), ())), mode)


def tn(a, b, mode=None):
    return dot(a, b, (((0,), (0,)), ((), ())), mode)


def iota(dim, shape=(TOK, TOK)):
    return lax.broadcasted_iota(jnp.int32, shape, dim)


def sigmoid(v):
    return 1.0 / (1.0 + jnp.exp(-v))


def softplus(v):
    e = jnp.exp(-jnp.abs(v))
    u = 1.0 + e
    tail = jnp.where(u == 1.0, e, jnp.log(u) * e / jnp.where(u == 1.0, 1.0, u - 1.0))
    return jnp.maximum(v, 0.0) + tail


def lanes(sm, first, count):
    return jnp.concatenate(
        [sm[half, r : r + 1, :] for half in range(2) for r in range(first, first + count)],
        axis=1,
    )


def decay_weights(sm):
    rows = [lanes(sm, R_WD + 4 * i, 4) for i in range(8)]
    rows.append(jnp.zeros((TOK - 8, WIDTH), F32))
    return jnp.concatenate(rows, axis=0).astype(BF16)


def layout(lens, owner, replica):
    i, j = iota(0), iota(1)
    owned = (owner == replica).astype(F32)
    held = lens.astype(F32) * owned
    ends = jnp.sum(jnp.where(j <= i, held, 0.0), axis=1, keepdims=True)
    owned_col = jnp.sum(jnp.where(j == i, owned, 0.0), axis=1, keepdims=True)
    done = jnp.where(ends <= j.astype(F32), owned_col, 0.0)
    seg_row = jnp.sum(done, axis=0, keepdims=True)
    seg_col = jnp.sum(jnp.where(j == i, seg_row, 0.0), axis=1, keepdims=True)
    total = jnp.sum(held, axis=1, keepdims=True)
    t = iota(0, (TOK, 1)).astype(F32)
    usable = (t < total).astype(F32)
    return seg_col, seg_row, usable


def links(seg_col):
    wide = jnp.broadcast_to(seg_col, (TOK, TOK))
    t = iota(0)
    return [
        ((pltpu.roll(wide, d, 0) == wide) & (t >= d)).astype(F32)[:, :1] for d in range(1, TAPS)
    ]


def conv_tile(sig, taps_rows, link):
    out = sig * taps_rows[TAPS - 1]
    for d in range(1, TAPS):
        out = out + pltpu.roll(sig, d, 0) * link[d - 1] * taps_rows[TAPS - 1 - d]
    return out


def norm_rows(v):
    return lax.rsqrt(jnp.mean(v * v, axis=-1, keepdims=True) + EPS)


def decays(dec, sm):
    alog = sm[0, R_ALOG : R_ALOG + 1, :] + sm[1, R_ALOG : R_ALOG + 1, :]
    bias = sm[0, R_BIAS : R_BIAS + 1, :] + sm[1, R_BIAS : R_BIAS + 1, :]
    z = dec + bias
    rate = -jnp.exp(alog)
    logdecay = rate * softplus(z)
    tri = (iota(1) <= iota(0)).astype(F32)
    summed = nn(tri, logdecay, HI)
    return z, rate, logdecay, summed, sigmoid(dec)


def inverse(systems):
    i, j = iota(0), iota(1)
    eye = (i == j).astype(F32)
    low = i > j
    found = [eye - jnp.where(low & ((i // 2) == (j // 2)), a, 0.0) for a in systems]
    size = 2
    while size < TOK:
        mask = low & ((i // (2 * size)) == (j // (2 * size))) & ((i // size) != (j // size))
        inner = [nn(jnp.where(mask, a, 0.0), m, M_INV) for a, m in zip(systems, found)]
        found = [m - nn(m, b, M_INV) for m, b in zip(found, inner)]
        size *= 2
    return found


def head_inputs(proj, taps, link, h):
    out = []
    for first, width in (
        (KEY_DIM * h, KEY_DIM),
        (HEADS * KEY_DIM + KEY_DIM * h, KEY_DIM),
        (2 * HEADS * KEY_DIM + VALUE_DIM * h, VALUE_DIM),
    ):
        rows = [t[:, first : first + width] for t in taps]
        out.append((first, width, rows, conv_tile(proj[:, first : first + width], rows, link)))
    return out


WEIGHT_SHAPES = ((WIDTH, PROJ), (WIDTH, WIDTH), (WIDTH, 2 * HIDDEN_FF), (HIDDEN_FF, WIDTH))


def forward_body(
    x_ref, sm_ref, rows_of, out_ref, proj_ref, dec_ref, inv_ref, mid_ref, gu_ref,
    w_in, w_out, w_ff, w_down, mixed_ref, hid_ref, hook,
):
    seg_col, seg_row, _ = rows_of
    link = links(seg_col)
    same = (seg_col == seg_row).astype(F32)
    xf = x_ref[...].astype(F32)
    normed = (xf * norm_rows(xf) * lanes(sm_ref, R_GIN, 4)).astype(BF16)
    dec = nt(normed, decay_weights(sm_ref))
    dec_ref[...] = dec
    hook("in")

    for c in range(0, PROJ, 512):
        proj_ref[:, c : c + 512] = nn(normed, w_in[:, c : c + 512])

    z, rate, logdecay, summed, beta = decays(dec, sm_ref)
    summed_t = summed.T
    taps = [lanes(sm_ref, R_TAPS + 8 * k, 8) for k in range(TAPS)]
    i, j = iota(0), iota(1)
    strict = i > j
    kept, systems = [], []
    for h in range(HEADS):
        (_, _, _, qc), (_, _, _, kc), (_, _, _, vc) = head_inputs(proj_ref, taps, link, h)
        q, k, v = (c * sigmoid(c) for c in (qc, kc, vc))
        q = q * lax.rsqrt(jnp.sum(q * q, axis=-1, keepdims=True) + EPS) * KEY_DIM ** (-0.5)
        k = k * lax.rsqrt(jnp.sum(k * k, axis=-1, keepdims=True) + EPS)
        w = jnp.exp(jnp.minimum(summed[:, h : h + 1] - summed_t[h : h + 1, :], 0.0)) * same
        b = beta[:, HEADS + h : HEADS + h + 1]
        gram = nt(k, k, M_FWD)
        systems.append(jnp.where(strict, b * gram * w, 0.0))
        scores = jnp.where(i >= j, nt(q, k, M_FWD) * w, 0.0)
        kept.append((scores, b * v))
        hook(h)
    inv = inverse(systems)
    hook("inverse")
    gain_out = lanes(sm_ref, R_GOUT, 1)
    for h in range(HEADS):
        inv_ref[h] = inv[h]
        scores, bv = kept[h]
        delta = nn(scores, nn(inv[h], bv, M_FWD), M_FWD)
        cols = slice(VALUE_DIM * h, VALUE_DIM * (h + 1))
        gate = proj_ref[:, CONV + VALUE_DIM * h : CONV + VALUE_DIM * (h + 1)]
        mixed_ref[:, cols] = (
            delta * norm_rows(delta) * gain_out * (gate * sigmoid(gate))
        ).astype(BF16)
    hook("out")
    mid = xf + nn(mixed_ref[...], w_out[...])
    mid_ref[...] = mid
    normed_ff = (mid * norm_rows(mid) * lanes(sm_ref, R_GFF, 4)).astype(BF16)
    hook("ff")

    for first in range(0, HIDDEN_FF, 256):
        width = min(256, HIDDEN_FF - first)
        a = slice(first, first + width)
        b = slice(HIDDEN_FF + first, HIDDEN_FF + first + width)
        gate = nn(normed_ff, w_ff[:, a])
        up = nn(normed_ff, w_ff[:, b])
        gu_ref[:, a] = gate
        gu_ref[:, b] = up
        hid_ref[:, a] = (gate * sigmoid(gate) * up).astype(BF16)

    hook("down")
    out_ref[...] = (mid + nn(hid_ref[...], w_down[...])).astype(BF16)


def backward_body(
    x_ref, cot_ref, sm_ref, rows_of,
    proj_ref, dec_ref, inv_ref, mid_ref, gu_ref,
    dx_ref, small_ref, nrm_t, mix_t, nff_t, hid_t, dproj_ref, dmid_ref, dgu_ref, dout_ref,
    w_in, w_out, w_ff, w_down, dmix_ref, hook,
):
    i, j = iota(0), iota(1)
    seg_col, seg_row, _ = rows_of
    link = links(seg_col)
    same = (seg_col == seg_row).astype(F32)
    dout = cot_ref[...].astype(F32)
    doutb = dout.astype(BF16)
    dout_ref[...] = doutb
    small_ref[...] = jnp.zeros_like(small_ref)

    for first in range(0, HIDDEN_FF, 256):
        width = min(256, HIDDEN_FF - first)
        a = slice(first, first + width)
        b = slice(HIDDEN_FF + first, HIDDEN_FF + first + width)
        gate, up = gu_ref[:, a], gu_ref[:, b]
        sg = sigmoid(gate)
        d_hidden = nt(doutb, w_down[a, :])
        dgu_ref[:, a] = (d_hidden * up * sg * (1.0 + gate * (1.0 - sg))).astype(BF16)
        dgu_ref[:, b] = (d_hidden * gate * sg).astype(BF16)
        hid_t[a, :] = (gate * sg * up).T.astype(BF16)
    mid = mid_ref[...]
    r = norm_rows(mid)
    n = mid * r
    gain_ff = lanes(sm_ref, R_GFF, 4)
    nff_t[...] = (n * gain_ff).T.astype(BF16)
    hook("ff")

    for c in range(0, WIDTH, 256):
        dmix_ref[:, c : c + 256] = nt(dgu_ref[...], w_ff[c : c + 256, :])

    d = dmix_ref[...]
    put(small_ref, R_GFF, 4, jnp.sum(d * n, axis=0, keepdims=True))
    d = d * gain_ff
    dmid = dout + r * (d - n * jnp.mean(d * n, axis=-1, keepdims=True))
    dmidb = dmid.astype(BF16)
    dmid_ref[...] = dmidb
    dmix_ref[...] = nt(dmidb, w_out[...])

    z, rate, logdecay, summed, beta = decays(dec_ref[...], sm_ref)
    summed_t = summed.T
    taps = [lanes(sm_ref, R_TAPS + 8 * k, 8) for k in range(TAPS)]
    gain_out = lanes(sm_ref, R_GOUT, 1)
    strict, causal = i > j, i >= j
    d_gain_out = jnp.zeros((1, VALUE_DIM), F32)
    d_col = jnp.zeros((TOK, TOK), F32)
    d_row = jnp.zeros((TOK, TOK), F32)
    for h in range(HEADS):
        parts = head_inputs(proj_ref, taps, link, h)
        sig = [sigmoid(p[3]) for p in parts]
        qa, ka, v = (p[3] * s for p, s in zip(parts, sig))
        rq = lax.rsqrt(jnp.sum(qa * qa, axis=-1, keepdims=True) + EPS)
        rk = lax.rsqrt(jnp.sum(ka * ka, axis=-1, keepdims=True) + EPS)
        q = qa * rq * KEY_DIM ** (-0.5)
        k = ka * rk
        w = jnp.exp(jnp.minimum(summed[:, h : h + 1] - summed_t[h : h + 1, :], 0.0)) * same
        b = beta[:, HEADS + h : HEADS + h + 1]
        gram = nt(k, k, M_FWD)
        qk = nt(q, k, M_FWD)
        ws = jnp.where(strict, w, 0.0)
        wc = jnp.where(causal, w, 0.0)
        scores = qk * wc
        inv = inv_ref[h]
        u = nn(inv, b * v, M_FWD)
        delta = nn(scores, u, M_FWD)
        gcols = slice(CONV + VALUE_DIM * h, CONV + VALUE_DIM * (h + 1))
        vcols = slice(VALUE_DIM * h, VALUE_DIM * (h + 1))
        gate = proj_ref[:, gcols]
        sg = sigmoid(gate)
        si = gate * sg
        rd = norm_rows(delta)
        nd = delta * rd
        dm = dmix_ref[:, vcols]
        mix_t[vcols, :] = (nd * gain_out * si).T.astype(BF16)
        dproj_ref[:, gcols] = (dm * nd * gain_out * sg * (1.0 + gate * (1.0 - sg))).astype(BF16)
        dn = dm * si
        d_gain_out = d_gain_out + jnp.sum(dn * nd, axis=0, keepdims=True)
        dn = dn * gain_out
        ddelta = rd * (dn - nd * jnp.mean(dn * nd, axis=-1, keepdims=True))
        dscores = nt(ddelta, u, 3)
        du = tn(scores, ddelta, 3)
        dr = tn(inv, du, 3)
        da = -nt(dr, u, 3)
        dqk = dscores * wc
        dgram = da * b * ws
        pair = dqk * qk + dgram * gram
        dq = nn(dqk, k, M_BWD)
        dk = tn(dqk, q, M_BWD) + nn(dgram + dgram.T, k, M_BWD)
        dv = b * dr
        dbeta = jnp.sum(da * gram * ws, axis=1, keepdims=True) + jnp.sum(
            dr * v, axis=1, keepdims=True
        )
        d_col = jnp.where(j == h, jnp.sum(pair, axis=1, keepdims=True), d_col)
        d_col = jnp.where(j == HEADS + h, dbeta, d_col)
        d_row = jnp.where(i == h, jnp.sum(pair, axis=0, keepdims=True), d_row)
        dq = KEY_DIM ** (-0.5) * dq
        dqa = rq * dq - qa * (rq * rq * rq) * jnp.sum(dq * qa, axis=-1, keepdims=True)
        dka = rk * dk - ka * (rk * rk * rk) * jnp.sum(dk * ka, axis=-1, keepdims=True)
        for (first, width, rows, c), s, dact in zip(parts, sig, (dqa, dka, dv)):
            dc = dact * s * (1.0 + c * (1.0 - s))
            raw = proj_ref[:, first : first + width]
            total = dc * rows[TAPS - 1]
            put_taps(small_ref, TAPS - 1, first, jnp.sum(dc * raw, axis=0, keepdims=True))
            for dist in range(1, TAPS):
                dcl = dc * link[dist - 1]
                put_taps(
                    small_ref, TAPS - 1 - dist, first,
                    jnp.sum(dcl * pltpu.roll(raw, dist, 0), axis=0, keepdims=True),
                )
                total = total + pltpu.roll(dcl, TOK - dist, 0) * rows[TAPS - 1 - dist]
            dproj_ref[:, first : first + width] = total.astype(BF16)
        hook(h)
    put(small_ref, R_GOUT, 1, d_gain_out)
    d_summed = d_col - d_row.T
    later = (j >= i).astype(F32)
    dlog = nn(later, d_summed, HI)
    dz = dlog * rate * sigmoid(z)
    head_lane = j < HEADS
    d_alog = jnp.sum(jnp.where(head_lane, dlog * logdecay, 0.0), axis=0, keepdims=True)
    d_bias = jnp.sum(jnp.where(head_lane, dz, 0.0), axis=0, keepdims=True)
    for half in range(2):
        small_ref[half, R_ALOG : R_ALOG + 1, :] = d_alog
        small_ref[half, R_BIAS : R_BIAS + 1, :] = d_bias
    ddec = jnp.where(
        head_lane, dz, jnp.where(j < 2 * HEADS, d_col * beta * (1.0 - beta), 0.0)
    ).astype(BF16)

    xf = x_ref[...].astype(F32)
    r = norm_rows(xf)
    n = xf * r
    gain_in = lanes(sm_ref, R_GIN, 4)
    normed = (n * gain_in).astype(BF16)
    nrm_t[...] = (n * gain_in).T.astype(BF16)
    hook("mixer")
    gwd = tn(ddec, normed)
    for row in range(2 * HEADS):
        put(small_ref, R_WD + 4 * row, 4, gwd[row : row + 1, :])

    for c in range(0, WIDTH, 256):
        dmix_ref[:, c : c + 256] = nt(dproj_ref[...], w_in[c : c + 256, :])

    d = dmix_ref[...] + nn(ddec, decay_weights(sm_ref))
    put(small_ref, R_GIN, 4, jnp.sum(d * n, axis=0, keepdims=True))
    d = d * gain_in
    dx_ref[...] = (dmid + r * (d - n * jnp.mean(d * n, axis=-1, keepdims=True))).astype(BF16)


def put(ref, first, count, row):
    for half in range(2):
        for c in range(count):
            at = (half * count + c) * 128
            ref[half, first + c : first + c + 1, :] = row[:, at : at + 128]


def put_taps(ref, tap, first, row):
    for c in range(row.shape[1] // 128):
        block = first // 128 + c
        at = R_TAPS + 8 * tap + block % 8
        ref[block // 8, at : at + 1, :] = row[:, c * 128 : c * 128 + 128]


ORDERS = ((0, 1, 2, 3), (1, 0, 3, 2), (2, 3, 0, 1), (3, 2, 1, 0))
FLAT = (
    (2, 0, 256, 1, False),
    (2, 256, 768, 3, True),
    (2, 1024, 768, 2, False),
    (2, 1792, 1024, 1, True),
    (3, 0, 1024, 0, False),
    (0, 0, 1024, 3, False),
    (0, 1024, 1024, 1, False),
    (0, 2048, 768, 2, False),
    (0, 2816, 256, 2, False),
    (1, 0, 512, 0, True),
    (1, 512, 512, 2, True),
)
ORDER = (
    (5, 0), (6, 0), (7, 0), (8, 0), (9, 0), (10, 0), (0, 1), (11, 0), (1, 1), (2, 1), (11, 1),
    (5, 1), (4, 1), (6, 1), (7, 1), (0, 2), (3, 1), (1, 2), (8, 1), (11, 2), (2, 2), (9, 1),
    (6, 2), (5, 2), (4, 2), (2, 3), (7, 2), (1, 3), (0, 3), (10, 1), (8, 2), (9, 2), (3, 2),
    (4, 3), (0, 4), (7, 3), (6, 3), (8, 3), (0, 5), (10, 2), (4, 4), (5, 3), (3, 3), (6, 4),
    (0, 6), (11, 3), (2, 4), (1, 4), (10, 3), (4, 5), (6, 5), (5, 4), (2, 5), (9, 3), (3, 4),
    (0, 7), (1, 5), (7, 4), (8, 4), (10, 4), (4, 6), (6, 6), (5, 5), (2, 6), (9, 4), (0, 8),
    (7, 5), (3, 5), (8, 5), (10, 5), (1, 6), (11, 4), (5, 6), (6, 7), (4, 7), (9, 5), (2, 7),
    (0, 9), (3, 6), (7, 6), (8, 6), (10, 6), (9, 6), (1, 7), (5, 7), (6, 8), (2, 8), (9, 7),
    (11, 5), (7, 7), (8, 7), (3, 7), (10, 7), (1, 8), (4, 8), (7, 8), (5, 8), (8, 8), (3, 8),
    (10, 8), (6, 9), (2, 9), (9, 8), (1, 9), (4, 9), (7, 9), (8, 9), (3, 9), (9, 9), (5, 9),
    (10, 9),
)

GATHER = (
    (2, 0, 768, 0, True), (2, 768, 768, 1, True), (2, 1536, 768, 3, True), (2, 2304, 512, 2, True),
    (3, 0, 1024, 2, False), (0, 0, 1024, 0, False), (0, 1024, 1024, 1, False),
    (0, 2048, 1024, 3, False), (1, 0, 256, 0, False), (1, 256, 512, 1, False),
    (1, 768, 256, 3, False),
)
DOWN = 3


class Place:
    def __init__(self):
        self.section = lax.axis_index("section")
        dp = lax.axis_index("dp")
        self.half = lax.axis_index("fsdp")
        x, z, core = dp // 8, (dp // 2) % 4, dp % 2
        self.core = core

        def at(x, z, core, half):
            return (self.section, (x * 4 + z) * 2 + core, half)

        xa, za = x + 1 - 2 * (x % 2), z + 1 - 2 * (z % 2)
        self.links = (
            at(xa, z, core, self.half),
            at(3 - x, z, core, self.half),
            at(x, za, core, self.half),
            at(x, 3 - z, core, self.half),
        )
        self.sibling = at(x, z, 1 - core, self.half)
        self.pair = at(x, z, core, 1 - self.half)
        self.other = (1 - self.section, dp, self.half)
        self.bits = ((x % 2 + x // 2) % 2, x // 2, (z % 2 + z // 2) % 2, z // 2)

    def greet(self, *more):
        barrier = pltpu.get_barrier_semaphore()
        everyone = (*self.links, self.sibling, self.pair, *more)
        for device in everyone:
            pl.semaphore_signal(
                barrier, inc=1, device_id=device, device_id_type=pl.DeviceIdType.MESH
            )
        pl.semaphore_wait(barrier, len(everyone))


class Chunk:
    def __init__(self, place, weight, first, width, flavor, pair_first=False):
        self.pair_first = pair_first
        self.weight, self.first, self.width, self.order = weight, first, width, ORDERS[flavor]
        self.bits = [place.bits[d] for d in self.order]
        self.partners = [place.links[d] for d in self.order]
        self.rows = 352 if weight == DOWN else 256

    def size(self, steps):
        if self.weight == DOWN:
            return (self.rows >> min(steps, 1), self.width >> max(steps - 1, 0))
        return (self.rows >> steps, self.width)

    def start(self, steps, other=False):
        row = col = 0
        for k in range(1, steps + 1):
            bit = self.bits[k - 1]
            if other and k == steps:
                bit = 1 - bit
            if self.weight == DOWN and k > 1:
                col = col + bit * self.size(k)[1]
            else:
                row = row + bit * self.size(k)[0]
        return row, col

    def window(self, steps, other=False, row0=0, col0=0):
        (row, col), (rows, cols) = self.start(steps, other), self.size(steps)
        row, col = row + row0, col + col0
        if not isinstance(row, int):
            row = pl.multiple_of(row, 16)
        if not isinstance(col, int):
            col = pl.multiple_of(col, 128)
        return pl.ds(row, rows), pl.ds(col, cols)


def send(src, dst, sems, k, device):
    copy = pltpu.make_async_remote_copy(
        src_ref=src, dst_ref=dst, send_sem=sems[0].at[k], recv_sem=sems[1].at[k],
        device_id=device, device_id_type=pl.DeviceIdType.MESH,
    )
    copy.start()
    return copy


HALF_ROWS = (512, 512, 512, 704)
COLUMNS = (PROJ, WIDTH, 2 * HIDDEN_FF, WIDTH)


GATHER_FLAT = tuple(
    c[:4] for c in sorted(GATHER, key=lambda c: (0, 3, 1, 2)[c[0]])
)
PACKED = 0
STAGES = 6


def layers_kernel(
    x_ref, cot_ref, mask_ref, lens_ref, own_ref,
    gin_ref, gff_ref, gout_ref, taps_ref, wdec_ref, alog_ref, bias_ref, wi, wo, wf, wd,
    out_ref, dx_ref, tot_ref, g_in, g_out, g_ff, g_down,
    small_ref, nrm_t, mix_t, nff_t, hid_t, dproj_ref, dmid_ref, dgu_ref, dout_ref,
    w_in, w_out, w_ff, w_down, sm_ref, pk_wide, pk_ref, pk_far, proj_ref, dec_ref, inv_ref,
    mid_ref, gu_ref, mixed_ref, hid_ref, dmix_ref, xin_ref, next_ref, cin_ref, back_ref,
    send_sem, recv_sem, local_sem, *scratch,
):
    place = Place()
    pk_wide[...] = jnp.zeros_like(pk_wide)
    for ref, first, per_row in (
        (gin_ref, R_GIN, 4), (gff_ref, R_GFF, 4), (gout_ref, R_GOUT, 1), (taps_ref, R_TAPS, 8),
        (wdec_ref, R_WD, 4),
    ):
        rows = ref[...].astype(F32)
        for r in range(rows.shape[0]):
            for c in range(per_row):
                at = first + r * per_row + c
                pk_wide[at : at + 1, :] = rows[r : r + 1, c * 128 : c * 128 + 128]
    for ref, at in ((alog_ref, R_ALOG), (bias_ref, R_BIAS)):
        two = ref[...].astype(F32)
        none = jnp.zeros((1, 2), F32)
        pk_wide[at : at + 1, 0:2] = jnp.where(place.half == 0, two, none)
        pk_wide[at : at + 1, 2:4] = jnp.where(place.half == 0, none, two)
    pk_ref[...] = pk_wide[...].astype(BF16)
    sems = (send_sem, recv_sem)
    shards, whole = (wi, wo, wf, wd), (w_in, w_out, w_ff, w_down)
    chunks = [Chunk(place, *c) for c in GATHER_FLAT]
    count = len(chunks)
    first = {w: [n for n, c in enumerate(chunks) if c.weight == w] for w in range(4)}

    def make(src, dst, k, device):
        return pltpu.make_async_remote_copy(
            src_ref=src, dst_ref=dst, send_sem=sems[0].at[k], recv_sem=sems[1].at[k],
            device_id=device, device_id_type=pl.DeviceIdType.MESH,
        )

    def local(w):
        rows = HALF_ROWS[w]
        at = pl.ds(pl.multiple_of(place.half * rows, 16), rows)
        return pltpu.make_async_copy(shards[w], whole[w].at[at, :], local_sem.at[w])

    def stage_copy(n, stage):
        c = chunks[n]
        w, rows = c.weight, HALF_ROWS[c.weight]
        k = 1 + stage * count + n
        if stage == 0:
            src = shards[w].at[c.window(4, row0=place.core * c.rows, col0=c.first)]
            to = c.window(4, row0=place.half * rows + place.core * c.rows, col0=c.first)
            return make(src, whole[w].at[to], k, place.pair)
        row0 = (1 - place.half) * rows + place.core * c.rows
        block = whole[w].at[c.window(5 - stage, row0=row0, col0=c.first)]
        device = c.partners[4 - stage] if stage < 5 else place.sibling
        return make(block, block, k, device)

    def passed_on(ns, stage):
        for n in ns:
            stage_copy(n, stage - 1).wait_recv()
            stage_copy(n, stage).start()

    rest = first[1] + first[2] + first[3]

    def complete(w):
        for n in first[w]:
            stage_copy(n, STAGES - 1).wait_recv()
        local(w).wait()

    def gather_hook(point):
        if point == "in":
            for stage in range(1, 4):
                passed_on(first[0], stage)
                if stage == 1:
                    passed_on(rest, 1)
            passed_on(first[0], 4)
            passed_on(rest, 2)
            passed_on(first[0], 5)
            complete(0)
        elif point == 0:
            passed_on(rest, 3)
        elif point == 2:
            passed_on(rest, 4)
        elif point == "inverse":
            passed_on(rest, 5)
        elif point in ("out", "ff", "down"):
            complete({"out": 1, "ff": 2, "down": 3}[point])

    place.greet(place.other)
    packed = make(pk_ref, pk_far, PACKED, place.pair)
    packed.start()
    for w in (0, 1, 2, 3):
        for n in first[w]:
            stage_copy(n, 0).start()
        local(w).start()
    rows_of = layout(lens_ref[...], own_ref[...], lax.axis_index("dp") * 2 + place.half)
    packed.wait()
    sm_ref[place.half] = pk_ref[...].astype(F32)
    sm_ref[1 - place.half] = pk_far[...].astype(F32)
    xin_ref[...] = x_ref[...]
    forth = make(out_ref, next_ref, 1 + STAGES * count, place.other)
    back = make(dx_ref, back_ref, 2 + STAGES * count, place.other)
    section = place.section

    @pl.loop(0, 2)
    def _(turn):
        def hook(point):
            @pl.when(turn == 0)
            def _():
                gather_hook(point)

        forward_body(
            xin_ref, sm_ref, rows_of, out_ref, proj_ref, dec_ref, inv_ref, mid_ref, gu_ref,
            w_in, w_out, w_ff, w_down, mixed_ref, hid_ref, hook,
        )

        @pl.when(turn == 0)
        def _():
            forth.start()
            forth.wait()
            xin_ref[...] = jnp.where(section == 0, x_ref[...], next_ref[...])

    mask = jnp.sum(
        jnp.where(iota(0) == iota(1), mask_ref[...].astype(F32), 0.0), axis=1, keepdims=True
    )
    cin_ref[...] = (cot_ref[...].astype(F32) * (mask * rows_of[2])).astype(BF16)

    cross, event, small_step, close, sums = reducer(
        place, (nrm_t, mix_t, nff_t, hid_t), (dproj_ref, dmid_ref, dgu_ref, dout_ref),
        (g_in, g_out, g_ff, g_down), scratch,
    )

    def reduce_hook(point):
        if point == "ff":
            cross(2)
            cross(3)
        elif point == 0:
            event(0, 0)
            event(1, 0)
        elif point == 1:
            event(2, 0)
            event(3, 0)
        elif point == 2:
            event(4, 0)
        elif point == "mixer":
            cross(0)
            cross(1)

    for turn in range(2):
        backward_body(
            xin_ref, cin_ref, sm_ref, rows_of,
            proj_ref, dec_ref, inv_ref, mid_ref, gu_ref,
            dx_ref, small_ref, nrm_t, mix_t, nff_t, hid_t, dproj_ref, dmid_ref, dgu_ref, dout_ref,
            w_in, w_out, w_ff, w_down, dmix_ref, reduce_hook if turn else (lambda point: None),
        )
        if turn == 0:
            back.start()
            back.wait()
            cin_ref[...] = jnp.where(section == 0, back_ref[...], cin_ref[...])

    sums[0] = small_ref[...]
    for n, stage in ORDER:
        if n == len(FLAT):
            small_step()
        else:
            event(n, stage)
    close(tot_ref)
    for n in range(count):
        for stage in range(STAGES):
            stage_copy(n, stage).wait_send()


def layers(x, cot, mask, lens, own, smalls, weights):
    vm = pl.BlockSpec(memory_space=pltpu.VMEM)
    hbm = pl.BlockSpec(memory_space=pl.ANY)
    tokens = (TOK, WIDTH)
    outs = [(tokens, BF16), (tokens, BF16), ((PACK, 128), F32)]
    outs += [((r, c), BF16) for r, c in zip(HALF_ROWS, COLUMNS)]
    scratch = [
        ((2, PACK, 128), F32), ((WIDTH, TOK), BF16), ((WIDTH, TOK), BF16), ((WIDTH, TOK), BF16),
        ((HIDDEN_FF, TOK), BF16), ((TOK, PROJ), BF16), (tokens, BF16),
        ((TOK, 2 * HIDDEN_FF), BF16), (tokens, BF16),
    ]
    scratch += [(s, BF16) for s in WEIGHT_SHAPES] + [
        ((2, PACK, 128), F32), ((PACK, 128), F32), ((PACK, 128), BF16), ((PACK, 128), BF16),
        ((TOK, PROJ), F32), ((TOK, TOK), F32), ((HEADS, TOK, TOK), F32), (tokens, F32),
        ((TOK, 2 * HIDDEN_FF), F32), (tokens, BF16), ((TOK, HIDDEN_FF), BF16), (tokens, F32),
        (tokens, BF16), (tokens, BF16), (tokens, BF16), (tokens, BF16),
    ]
    count = 3 + STAGES * len(GATHER_FLAT)
    return pl.pallas_call(
        layers_kernel,
        name="layers_and_sums",
        out_shape=[jax.ShapeDtypeStruct(s, d) for s, d in outs],
        in_specs=[vm] * 12 + [hbm] * 4,
        out_specs=[vm] * 3 + [hbm] * 4,
        scratch_shapes=[pltpu.VMEM(s, d) for s, d in scratch]
        + [
            pltpu.SemaphoreType.DMA((count,)),
            pltpu.SemaphoreType.DMA((count,)),
            pltpu.SemaphoreType.DMA((4,)),
        ]
        + reducer_scratch(),
        compiler_params=pltpu.CompilerParams(
            collective_id=1, has_side_effects=True, vmem_limit_bytes=VMEM_LIMIT
        ),
    )(x, cot, mask, lens, own, *smalls, *weights)


def reducer(place, lhs, rhs, grads, scratch):
    peer_l, peer_r = scratch[0:4], scratch[4:8]
    count = len(FLAT)
    parts, fins = scratch[8 : 8 + count], scratch[8 + count : 8 + 2 * count]
    scratch = scratch[8 + 2 * count :]
    arrived = [scratch[5 * n : 5 * n + 5] for n in range(count)]
    sums, sums_in, sums_pair, send_sem, recv_sem, local_sem = scratch[5 * count :]
    sems = (send_sem, recv_sem)
    ids = iter(range(10 * count + 18))
    chunks = [Chunk(place, *c) for c in FLAT]
    last, local, sent = {}, {}, []
    crossing = {}

    def cross(w):
        rows = peer_l[w].shape[1]
        found = []
        for h in range(2):
            at = pl.multiple_of(HALF_ROWS[w] * h + (1 - place.core) * rows, 16)
            found.append(
                send(lhs[w].at[pl.ds(at, rows), :], peer_l[w].at[h], sems, next(ids), place.sibling)
            )
        found.append(send(rhs[w], peer_r[w], sems, next(ids), place.sibling))
        sent.extend(found)
        crossing[w] = found


    def product(n, first):
        c = chunks[n]
        w = c.weight
        if c.pair_first:
            half = 1 - place.half if first else place.half
            blocks, rows = [(half, 0)], c.rows
        else:
            offset = pl.multiple_of(c.start(1, first)[0], 16)
            blocks, rows = [(0, offset), (1, offset)], c.size(1)[0]
        left = []
        for h, offset in blocks:
            at = pl.multiple_of(HALF_ROWS[w] * h + place.core * c.rows + offset, 16)
            left.append(
                jnp.concatenate(
                    [lhs[w][pl.ds(at, rows), :], peer_l[w][h, pl.ds(offset, rows), :]], axis=1
                )
            )
        both = left[0] if len(left) == 1 else jnp.concatenate(left, axis=0)
        for t in range(0, c.width, 256):
            cols = slice(c.first + t, c.first + t + 256)
            right = jnp.concatenate([rhs[w][:, cols], peer_r[w][:, cols]], axis=0)
            out = nn(both, right).astype(BF16)
            for k, (h, offset) in enumerate(blocks):
                parts[n][h, pl.ds(offset, rows), t : t + 256] = out[k * rows : (k + 1) * rows]

    def halves(n):
        return place.half if chunks[n].pair_first else slice(None)

    def give(n, step):
        c = chunks[n]
        at = c.window(step, other=True)
        last[n] = send(
            parts[n].at[halves(n), at[0], at[1]], arrived[n][step - 1], sems, next(ids),
            c.partners[step - 1],
        )
        sent.append(last[n])

    def add(n, step):
        c = chunks[n]
        (row, col), (rows, cols) = c.start(step), c.size(step)
        col = pl.ds(pl.multiple_of(col, 128), cols) if c.weight == DOWN else slice(None)
        lead = (slice(None),) if not c.pair_first else ()

        @pl.loop(0, rows // 16)
        def _(t):
            at = pl.ds(pl.multiple_of(row + t * 16, 16), 16)
            got = arrived[n][step - 1][(*lead, pl.ds(pl.multiple_of(t * 16, 16), 16), slice(None))]
            old = parts[n][halves(n), at, col]
            parts[n][halves(n), at, col] = (old.astype(F32) + got.astype(F32)).astype(BF16)

    def finish(n, block):
        c = chunks[n]
        fins[n][...] = block
        to = grads[c.weight].at[c.window(4, row0=place.core * c.rows, col0=c.first)]
        local[n] = pltpu.make_async_copy(fins[n], to, local_sem.at[n])
        local[n].start()
        last[n] = send(fins[n], to, sems, next(ids), c.partners[3])
        sent.append(last[n])

    def to_pair(n, src, dst):
        last[n] = send(src, dst, sems, next(ids), place.pair)
        sent.append(last[n])

    def event(n, stage):
        c = chunks[n]
        w = c.weight
        if stage == 0:
            for copy in crossing.pop(w, ()):
                copy.wait_recv()
            product(n, True)
            if c.pair_first:
                to_pair(n, parts[n].at[1 - place.half], arrived[n][4])
            else:
                give(n, 1)
            product(n, False)
        elif c.pair_first and stage == 1:
            last[n].wait_recv()

            @pl.loop(0, c.rows // 16)
            def _(t):
                at = pl.ds(pl.multiple_of(t * 16, 16), 16)
                old = parts[n][place.half, at, :].astype(F32)
                parts[n][place.half, at, :] = (old + arrived[n][4][at, :].astype(F32)).astype(BF16)

            give(n, 1)
        elif c.pair_first and stage <= 4:
            last[n].wait_recv()
            add(n, stage - 1)
            give(n, stage)
        elif c.pair_first and stage == 5:
            last[n].wait_recv()
            at = c.window(4)
            finish(
                n,
                (
                    parts[n][place.half, at[0], at[1]].astype(F32)
                    + arrived[n][3][...].astype(F32)
                ).astype(BF16),
            )
        elif stage <= 3:
            last[n].wait_recv()
            add(n, stage)
            give(n, stage + 1)
        elif stage == 4:
            last[n].wait_recv()
            add(n, 4)
            at = c.window(4)
            to_pair(n, parts[n].at[1 - place.half, at[0], at[1]], arrived[n][4])
        elif stage == 5:
            last[n].wait_recv()
            at = c.window(4)
            finish(
                n,
                (
                    parts[n][place.half, at[0], at[1]].astype(F32)
                    + arrived[n][4][...].astype(F32)
                ).astype(BF16),
            )
        elif stage <= 8:
            if stage == 6:
                local[n].wait()
            last[n].wait_recv()
            steps_left = 9 - stage
            block = grads[w].at[c.window(steps_left, row0=place.core * c.rows, col0=c.first)]
            last[n] = send(block, block, sems, next(ids), c.partners[steps_left - 1])
            sent.append(last[n])
        else:
            last[n].wait_recv()
            block = grads[w].at[c.window(0, row0=place.core * c.rows, col0=c.first)]
            last[n] = send(block, block, sems, next(ids), place.sibling)
            sent.append(last[n])

    small = []

    def small_step():
        steps = (place.sibling, *place.links)
        k = len(small)
        if 0 < k < 6:
            small[-1].wait_recv()
            sums[k] = sums[k - 1] + sums_in[k - 1]
        if k < 5:
            small.append(send(sums.at[k], sums_in.at[k], sems, next(ids), steps[k]))
        elif k == 5:
            small.append(
                send(sums.at[5, 1 - place.half], sums_pair, sems, next(ids), place.pair)
            )

    def close(tot_ref):
        while len(small) < 6:
            small_step()
        small[-1].wait_recv()
        tot_ref[...] = sums[5, place.half] + sums_pair[...]
        for n in range(count):
            last[n].wait_recv()
        for copy in sent + small:
            copy.wait_send()

    return cross, event, small_step, close, sums


class Sizes:
    bits = (0, 0, 0, 0)
    links = (None,) * 4


def reducer_scratch():
    chunks = [Chunk(Sizes, *c) for c in FLAT]
    count = len(FLAT)
    scratch = [pltpu.VMEM((2, r // 2, TOK), BF16) for r in HALF_ROWS]
    scratch += [pltpu.VMEM((TOK, c), BF16) for c in COLUMNS]
    scratch += [pltpu.VMEM((2, *c.size(0)), BF16) for c in chunks]
    scratch += [pltpu.VMEM(c.size(4), BF16) for c in chunks]
    for c in chunks:
        lead = () if c.pair_first else (2,)
        scratch += [pltpu.VMEM((*lead, *c.size(k)), BF16) for k in range(1, 5)]
        scratch.append(pltpu.VMEM(c.size(0 if c.pair_first else 4), BF16))
    total = 10 * count + 18
    scratch += [
        pltpu.VMEM((6, 2, PACK, 128), F32),
        pltpu.VMEM((5, 2, PACK, 128), F32),
        pltpu.VMEM((PACK, 128), F32),
        pltpu.SemaphoreType.DMA((total,)),
        pltpu.SemaphoreType.DMA((total,)),
        pltpu.SemaphoreType.DMA((count,)),
    ]
    return scratch


def finish_kernel(tot_ref, out_ref, dx_ref, *refs):
    sources, (o_gin, o_taps, o_wd, o_alog, o_bias, o_gout, o_gff) = refs[:4], refs[4:11]
    targets, o_out, o_dx = refs[11:15], refs[15], refs[16]
    narrow, wide = refs[17:21], refs[21:25]
    t_out, t_dx, in_sem, out_sem = refs[25:]
    half = lax.axis_index("fsdp")
    blocks = []
    for w, rows in enumerate(HALF_ROWS):
        size = rows // 4
        blocks += [(w, slice(k * size, (k + 1) * size)) for k in range(4)]
    loads = [
        pltpu.make_async_copy(sources[w].at[at], narrow[w].at[at], in_sem.at[k])
        for k, (w, at) in enumerate(blocks)
    ]
    for copy in loads:
        copy.start()
    tokens = ((out_ref, t_out, o_out), (dx_ref, t_dx, o_dx))
    passing = [
        pltpu.make_async_copy(src, via, in_sem.at[16 + k]) for k, (src, via, _) in enumerate(tokens)
    ]
    for copy in passing:
        copy.start()

    def row(first, count):
        return jnp.concatenate([tot_ref[first + k : first + k + 1, :] for k in range(count)], 1)

    o_gin[...] = row(R_GIN, 4)
    o_gff[...] = row(R_GFF, 4)
    o_gout[...] = row(R_GOUT, 1)
    for k in range(TAPS):
        o_taps[k : k + 1, :] = row(R_TAPS + 8 * k, 8)
    for k in range(2 * HEADS):
        o_wd[k : k + 1, :] = row(R_WD + 4 * k, 4)
    for ref, at in ((o_alog, R_ALOG), (o_bias, R_BIAS)):
        both = row(at, 1)
        ref[...] = jnp.where(half == 0, both[:, 0:2], both[:, 2:4])
    stores = []
    for k, (_, via, dst) in enumerate(tokens):
        passing[k].wait()
        stores.append(pltpu.make_async_copy(via, dst, out_sem.at[16 + k]))
        stores[-1].start()
    for k, (w, at) in enumerate(blocks):
        loads[k].wait()
        first, count = at.start, at.stop - at.start

        @pl.loop(0, count // 16)
        def _(t):
            here = pl.ds(pl.multiple_of(first + t * 16, 16), 16)
            wide[w][here, :] = narrow[w][here, :].astype(F32)

        copy = pltpu.make_async_copy(wide[w].at[at], targets[w].at[at], out_sem.at[k])
        copy.start()
        stores.append(copy)
    for copy in stores:
        copy.wait()


def finished(total, out, dx, grads):
    vm = pl.BlockSpec(memory_space=pltpu.VMEM)
    hbm = pl.BlockSpec(memory_space=pl.ANY)
    small = [(1, 512), (TAPS, 1024), (2 * HEADS, 512), (1, 2), (1, 2), (1, 128), (1, 512)]
    shapes = list(zip(HALF_ROWS, COLUMNS))
    return pl.pallas_call(
        finish_kernel,
        name="widen_gradients",
        out_shape=[jax.ShapeDtypeStruct(s, F32) for s in small + shapes]
        + [jax.ShapeDtypeStruct((TOK, WIDTH), BF16)] * 2,
        in_specs=[vm] + [hbm] * 6,
        out_specs=[vm] * 7 + [hbm] * 6,
        scratch_shapes=[pltpu.VMEM(s, BF16) for s in shapes]
        + [pltpu.VMEM(s, F32) for s in shapes]
        + [pltpu.VMEM((TOK, WIDTH), BF16)] * 2
        + [pltpu.SemaphoreType.DMA((18,)), pltpu.SemaphoreType.DMA((18,))],
        compiler_params=pltpu.CompilerParams(vmem_limit_bytes=VMEM_LIMIT),
    )(total, out, dx, *grads)


def on_device(
    inputs, out_grad, doc_lengths, doc_owner, loss_mask, gain_in, w_in, taps, w_decay, a_log,
    dt_bias, gain_out, w_out, gain_ff, w_ff_in, w_down,
):
    lens, own, mask = (a.reshape(1, TOK) for a in (doc_lengths, doc_owner, loss_mask))
    smalls = (gain_in, gain_ff, gain_out, taps[0].T, w_decay[0].T, a_log, dt_bias)
    mine = (w_in[0], w_out[0], w_ff_in[0], w_down[0])
    out, dx, total, *grads = layers(inputs, out_grad, mask, lens, own, smalls, mine)
    gin, g_taps, g_wd, g_alog, g_bias, g_gout, g_gff, g_in, g_out, g_ff, g_down, out, dx = finished(
        total, out, dx, grads
    )
    return (
        out[None], dx[None], gin, g_in[None], g_taps.T[None], g_wd.T[None], g_alog, g_bias, g_gout,
        g_out[None], g_gff, g_ff[None], g_down[None],
    )


def solution(mesh):
    tokens, pair = P(("dp", "fsdp"), None), P("section", "fsdp")
    matrix = P("section", "fsdp", None)
    params = (pair, matrix, matrix, matrix, pair, pair, pair, matrix, pair, matrix, matrix)
    return jax.shard_map(
        on_device,
        mesh=mesh,
        in_specs=(tokens, tokens, P(), P(), P(("dp", "fsdp")), *params),
        out_specs=(P("section", ("dp", "fsdp"), None),) * 2 + params,
        check_vma=False,
    )
```
